128 devices in a mesh: row: 8 (over z, y_hi), col: 16 (over y_lo, x, core).
Axes of the slice: x: 4, y: 4 (y_hi: 2, y_lo: 2; y = y_hi * 2 + y_lo), z: 4, core: 2. Of those that a mesh axis runs over, the one named last changes fastest.
Arguments:
- front: bfloat16 [16, 8, 128, 8, 16, 128], P(None, 'row', None, None, 'col'), may hold values from -8 to 25, as said below
- child_tiles: bfloat16 [16384, 128, 128], P(('row', 'col')), may hold values from -6 to 6
- tile_map: int32 [16384, 2], P(('row', 'col')), may hold values from 0 to 127, as said below
Outputs:
- factored: float32 [16, 8, 128, 8, 16, 128], P(None, 'row', None, None, 'col')
The draws below stay inside these ranges and needn't reach their ends.
Inputs may be any that keep to these rules, and one draw needn't show every extreme that they name: The leading 2048 x 2048 block of front is symmetric positive definite. `tile_map`: each row names a parent row tile outside the first 16 row tiles; column tiles may be any, the panel's included. The owner of tile (i, j) is the device at row i % 8 and column j % 16; the 128 tiles of one device send at most 2 tiles to any one owner, and in every draw some owner receives 2 tiles from every device.
All inputs are finite; a program needn't handle non-finite values.
Results may differ from the reference program's by a relative error of at most 0.0013.
Values may be sent and summed in bfloat16 or wider, within the bound.
No kernel may reach another device: no remote copies, remote signals or barrier semaphores. Data moves between devices by JAX's collectives and lax.ppermute only.
A program may use at most 384 MiB of HBM per device.

```python
import jax
import jax.numpy as jnp
from jax import lax

NF = 16384
PANEL = 2048
TILE = 128
CAP = 2
NT = 128
PT = 16
DEVS = 128
KTD = 128
N_ROW = 8
N_COL = 16


def draw_front(key, part):
    key = jax.random.fold_in(key, 11)
    keys = jax.random.split(key, 5)
    rest = NF - PANEL
    scales = jax.random.uniform(keys[0], (PANEL,), jnp.float32, 1.0, 2.0)
    spots = jax.random.uniform(keys[1], (PANEL,), jnp.float32) * 64.0
    upper = jnp.clip(jax.random.normal(keys[2], (PANEL, rest), jnp.float32), -6.0, 6.0)
    lower = 0.35 * jnp.clip(jax.random.normal(keys[3], (rest, PANEL), jnp.float32), -6.0, 6.0)
    trailing = jnp.clip(jax.random.normal(keys[4], (rest, rest), jnp.float32), -6.0, 6.0)
    kernel = scales[:, None] * scales[None, :] * jnp.exp(-jnp.abs(spots[:, None] - spots[None, :]))
    kernel = kernel + 20.0 * jnp.eye(PANEL, dtype=jnp.float32)
    whole = jnp.concatenate([jnp.concatenate([kernel, upper], 1), jnp.concatenate([lower, trailing], 1)], 0)
    return whole.reshape(NT // N_ROW, N_ROW, TILE, NT // N_COL, N_COL, TILE).astype(jnp.bfloat16)


def draw_tile_map(key, part):
    key = jax.random.fold_in(key, 5)
    keys = jax.random.split(key, 4)
    pair_count = DEVS * CAP
    weights = jax.random.randint(keys[0], (DEVS,), 0, 4) * 400
    busiest = jax.random.randint(keys[1], (), 0, DEVS)
    weights = jnp.where(jnp.arange(DEVS) == busiest, 4000, weights)
    offsets = jax.random.randint(keys[2], (DEVS,), 0, 1 << 20)
    pair_dest = jnp.arange(pair_count) // CAP
    rows_free = NT // N_ROW - PT // N_ROW
    cols_free = NT // N_COL - PT // N_COL
    cols_panel = PT // N_COL

    def one_sender(sender_key, sender):
        first_key, second_key = jax.random.split(sender_key)
        scores = (weights[pair_dest] + jax.random.randint(first_key, (pair_count,), 0, 1024)) * pair_count + jnp.arange(pair_count)
        _, chosen = lax.top_k(scores, KTD)
        chosen = jax.random.permutation(second_key, chosen)
        target = chosen // CAP
        within = chosen % CAP
        counter = sender * CAP + within + offsets[target]
        to_panel = counter % 4 == 0
        spot = counter % (rows_free * cols_free)
        spot_panel = counter // 4 % (rows_free * cols_panel)
        row_spot = jnp.where(to_panel, spot_panel // cols_panel, spot // cols_free)
        col_spot = jnp.where(to_panel, spot_panel % cols_panel, PT // N_COL + spot % cols_free)
        tile_row = (PT // N_ROW + row_spot) * N_ROW + target // N_COL
        tile_col = col_spot * N_COL + target % N_COL
        return jnp.stack([tile_row, tile_col], 1)
    result = jax.vmap(one_sender)(jax.random.split(keys[3], DEVS), jnp.arange(DEVS))
    return result.reshape(DEVS * KTD, 2).astype(jnp.int32)


def block_levels(key, dims, cuts, smallest, high):
    def one(dim, parts):
        draws = jax.random.uniform(jax.random.fold_in(jax.random.fold_in(key, 6), dim), (parts,), jnp.float32, smallest / len(cuts), high / len(cuts))
        return jnp.repeat(jnp.exp(draws), dims[dim] // parts).reshape((-1,) + (1,) * (len(dims) - dim - 1))

    factor_of = one(*cuts[0])
    for cut in cuts[1:]:
        factor_of = factor_of * one(*cut)
    return factor_of


def centred(own_key, shape, width, bound, cuts=(), kind=jnp.bfloat16):
    values = width * jax.random.normal(own_key, shape, jnp.float32)
    if cuts:
        values = values * block_levels(own_key, shape, cuts, -0.22, 0.18)
    return jnp.clip(values, -bound, bound).astype(kind)


def setup_inputs(seed: int = 0) -> dict:
    splits = jax.random.split(jax.random.key(seed), 4)
    return {
        "front": draw_front(jax.random.fold_in(splits[3], 71), 0),
        "child_tiles": centred(splits[1], (DEVS * KTD, TILE, TILE), 1.0, 6.0, ((0, 128),)),
        "tile_map": draw_tile_map(jax.random.fold_in(splits[3], 71), 0),
    }


def reference(front, child_tiles, tile_map):
    tiled = front.reshape(NT, TILE, NT, TILE).transpose(0, 2, 1, 3).astype(jnp.float32)
    blocks = child_tiles.reshape(DEVS, KTD, TILE, TILE)
    places = tile_map.reshape(DEVS, KTD, 2)

    def add_block(carry, item):
        pieces, where_to = item
        carry = carry.at[where_to[:, 0], where_to[:, 1]].add(pieces.astype(jnp.float32))
        return (carry, None)
    tiled, _ = lax.scan(add_block, tiled, (blocks, places))
    assembled = tiled.transpose(0, 2, 1, 3).reshape(NF, NF).astype(jnp.bfloat16)
    corner = assembled[:PANEL, :PANEL].astype(jnp.float32)
    lower_factor = jnp.linalg.cholesky(corner)
    below = lax.linalg.triangular_solve(lower_factor, assembled[PANEL:, :PANEL].astype(jnp.float32), left_side=False, lower=True, transpose_a=True)
    panel = jnp.concatenate([lower_factor, below], 0).astype(jnp.bfloat16)
    lower_rows = panel[PANEL:].astype(jnp.float32)
    trailing = assembled[PANEL:, PANEL:].astype(jnp.float32) - jnp.dot(lower_rows.astype(jnp.float32), lower_rows.T.astype(jnp.float32), preferred_element_type=jnp.float32)
    upper_zero = jnp.zeros((PANEL, NF - PANEL), jnp.float32)
    right_part = jnp.concatenate([upper_zero, trailing], 0)
    factored = jnp.concatenate([panel.astype(jnp.float32), right_part], 1)
    return factored.reshape(NT // N_ROW, N_ROW, TILE, NT // N_COL, N_COL, TILE)
```

```python
import jax
import jax.numpy as jnp
from jax import lax
from jax.experimental import pallas as pl
from jax.experimental.pallas import tpu as pltpu

from jax.sharding import PartitionSpec as P

CAP = 2
PANEL = 2048
TILE = 128
NT_DIMS = (((1,), (1,)), ((), ()))


def split2(x):
    hi = x.astype(jnp.bfloat16)
    lo = (x - hi.astype(jnp.float32)).astype(jnp.bfloat16)
    return hi, lo


def nt(a, b):
    return lax.dot_general(a, b, NT_DIMS, preferred_element_type=jnp.float32)


def invert_tile(a_ref, i_ref, out_ref):
    row = lax.broadcasted_iota(jnp.int32, (TILE, TILE), 0)
    col = lax.broadcasted_iota(jnp.int32, (TILE, TILE), 1)
    i_ref[...] = (row == col).astype(jnp.float32)
    full = (8, TILE)
    for g in range(TILE // 8):
        base = 8 * g
        group = a_ref[base : base + 8, :]
        cols = [jnp.broadcast_to(group[:, base + k : base + k + 1], full) for k in range(8)]
        d = {}
        for k in range(8):
            for i in range(k, 8):
                d[i, k] = jnp.broadcast_to(cols[k][i : i + 1, :], full)
        rs = {}
        lo = {}
        t = {}
        for j in range(8):
            rs[j] = lax.rsqrt(d[j, j])
            for i in range(j + 1, 8):
                lo[i, j] = d[i, j] * rs[j]
            for k in range(j + 1, 8):
                for i in range(k, 8):
                    d[i, k] = d[i, k] - lo[i, j] * lo[k, j]
            t[j, j] = rs[j]
            for m in range(j):
                acc = lo[j, m] * t[m, m]
                for k in range(m + 1, j):
                    acc = acc + lo[j, k] * t[k, m]
                t[j, m] = -(acc * rs[j])
        ga = [jnp.broadcast_to(a_ref[base + j : base + j + 1, :], full) for j in range(8)]
        gi = [jnp.broadcast_to(i_ref[base + j : base + j + 1, :], full) for j in range(8)]

        def lower(rows):
            out = []
            for i in range(8):
                acc = t[i, 0] * rows[0]
                for j in range(1, i + 1):
                    acc = acc + t[i, j] * rows[j]
                out.append(acc)
            return out

        def upper(rows):
            out = []
            for j in range(8):
                acc = t[7, j] * rows[7]
                for i in range(6, j - 1, -1):
                    acc = acc + t[i, j] * rows[i]
                out.append(acc)
            return out

        ui = lower(gi)
        for i in range(8):
            out_ref[base + i : base + i + 1, :] = ui[i][0:1, :]
        if g == TILE // 8 - 1:
            break
        va = upper(lower(ga))
        vi = upper(ui)
        for h in range(g + 1, TILE // 8):
            rows = slice(8 * h, 8 * h + 8)
            block = a_ref[rows, :]
            acc_a = block
            acc_i = i_ref[rows, :]
            for j in range(8):
                c = jnp.broadcast_to(block[:, base + j : base + j + 1], full)
                acc_a = acc_a - c * va[j]
                acc_i = acc_i - c * vi[j]
            a_ref[rows, :] = acc_a
            i_ref[rows, :] = acc_i


def factor_kernel(place_ref, tiles_ref, own_ref, xh_ref, xl_ref, m_ref, e_ref, f1_ref, f2_ref, a_ref, i_ref, t_ref):
    nt_ = PANEL // TILE
    half = nt_ // 2
    m_ref[...] = jnp.zeros_like(m_ref)
    for j in range(nt_):
        for i in range(j, nt_):
            m_ref[j // 2, i * TILE : (i + 1) * TILE, (j % 2) * TILE : (j % 2 + 1) * TILE] = tiles_ref[
                (i % 8) * 16 + j, i // 8
            ].astype(jnp.float32)
    own_ref[...] = jnp.zeros_like(own_ref)
    r = place_ref[0]
    c = place_ref[1]

    def step(k, carry):
        pair = k // 2
        lane = pl.multiple_of((k % 2) * TILE, TILE)
        top = pl.multiple_of(k * TILE, TILE)
        a_ref[...] = m_ref[pair, pl.ds(top, TILE), pl.ds(lane, TILE)]
        invert_tile(a_ref, i_ref, t_ref)
        row = lax.broadcasted_iota(jnp.int32, (TILE, TILE), 0)
        col = lax.broadcasted_iota(jnp.int32, (TILE, TILE), 1)
        th, tl = split2(t_ref[...])
        tt1 = jnp.concatenate([th, th], 1)
        tt2 = jnp.concatenate([tl, tl], 1)
        orig = m_ref[pair, pl.ds(top, TILE), pl.ds(lane, TILE)]
        oh, ol = split2(orig)
        oo = jnp.concatenate([oh, ol], 1)
        diag = nt(oo, tt1) + nt(oo, tt2)
        diag = jnp.where(row >= col, diag, 0.0).astype(jnp.bfloat16)
        m_ref[pair, pl.ds(top, TILE), pl.ds(lane, TILE)] = (row == col).astype(jnp.float32)

        for q in range(half):
            @pl.when(2 * q + 1 > k)
            def _():
                lane_tile = lax.broadcasted_iota(jnp.int32, (TILE, 2 * TILE), 1) // TILE + 2 * q
                m_ref[q, pl.ds(top, TILE), :] = jnp.where(
                    lane_tile > k, 0.0, m_ref[q, pl.ds(top, TILE), :]
                )

        def column(b, carry):
            rows = pl.ds(pl.multiple_of(b * 256, 256), 256)
            ch, cl = split2(m_ref[pair, rows, pl.ds(lane, TILE)])
            cc = jnp.concatenate([ch, cl], 1)
            e = nt(cc, tt1) + nt(cc, tt2)
            eh, el = split2(e)
            e_ref[rows, 0:TILE] = eh
            e_ref[rows, TILE:] = el
            tile = b * 2 + lax.broadcasted_iota(jnp.int32, (256, TILE), 0) // TILE
            zero = jnp.zeros((256, TILE), jnp.bfloat16)
            fh = jnp.where(tile > k, eh, zero)
            fl = jnp.where(tile > k, el, zero)
            f1_ref[rows, 0:TILE] = fh
            f1_ref[rows, TILE:] = fh
            f2_ref[rows, 0:TILE] = fl
            f2_ref[rows, TILE:] = fl
            xh_ref[rows, pl.ds(top, TILE)] = jnp.where(tile > k, zero, eh)
            xl_ref[rows, pl.ds(top, TILE)] = jnp.where(tile > k, zero, el)
            return carry

        lax.fori_loop(0, half, column, 0, unroll=True)

        @pl.when(k == c)
        def _():
            for a in range(2):
                i = r + a * 8
                src = e_ref[pl.ds(pl.multiple_of(i * TILE, TILE), TILE), 0:TILE]
                own_ref[a] = jnp.where(i == k, diag, jnp.where(i > k, src, jnp.zeros_like(src)))

        def update(q, carry):
            cols = pl.ds(pl.multiple_of(q * 256, 256), 256)
            f1 = f1_ref[cols, :]
            f2 = f2_ref[cols, :]
            for b in range(PANEL // 512):
                rows = pl.ds(b * 512, 512)
                ee = e_ref[rows, :]
                m_ref[q, rows, :] = m_ref[q, rows, :] - (nt(ee, f1) + nt(ee, f2))
            return carry

        lax.fori_loop((k + 1) // 2, half, update, 0)
        return carry

    lax.fori_loop(0, nt_, step, 0)


def factor_corner(tiles, place):
    vm = pl.BlockSpec(memory_space=pltpu.VMEM)
    return pl.pallas_call(
        factor_kernel,
        out_shape=(
            jax.ShapeDtypeStruct((2, TILE, TILE), jnp.bfloat16),
            jax.ShapeDtypeStruct((PANEL, PANEL), jnp.bfloat16),
            jax.ShapeDtypeStruct((PANEL, PANEL), jnp.bfloat16),
        ),
        in_specs=[pl.BlockSpec(memory_space=pltpu.SMEM), vm],
        out_specs=(vm, vm, vm),
        scratch_shapes=[
            pltpu.VMEM((8, PANEL, 256), jnp.float32),
            pltpu.VMEM((PANEL, 256), jnp.bfloat16),
            pltpu.VMEM((PANEL, 256), jnp.bfloat16),
            pltpu.VMEM((PANEL, 256), jnp.bfloat16),
            pltpu.VMEM((TILE, TILE), jnp.float32),
            pltpu.VMEM((TILE, TILE), jnp.float32),
            pltpu.VMEM((TILE, TILE), jnp.float32),
        ],
        compiler_params=pltpu.CompilerParams(vmem_limit_bytes=60 * 1024 * 1024),
        cost_estimate=pl.CostEstimate(flops=100_000_000_000, bytes_accessed=24_000_000, transcendentals=0),
        name="factor_corner",
    )(place, tiles)


def pack_kernel(slot_ref, child_ref, packed_ref, sem):
    count = child_ref.shape[0]

    def start(t, carry):
        pltpu.make_async_copy(child_ref.at[t], packed_ref.at[slot_ref[t]], sem).start()
        return carry

    lax.fori_loop(0, count, start, 0)
    pltpu.make_async_copy(child_ref, packed_ref.at[pl.ds(0, count)], sem).wait()


def pack(slots, child_tiles):
    count = child_tiles.shape[0]
    return pl.pallas_call(
        pack_kernel,
        out_shape=jax.ShapeDtypeStruct((CAP * count, TILE, TILE), jnp.bfloat16),
        in_specs=[pl.BlockSpec(memory_space=pltpu.SMEM), pl.BlockSpec(memory_space=pl.ANY)],
        out_specs=pl.BlockSpec(memory_space=pl.ANY),
        scratch_shapes=[pltpu.SemaphoreType.DMA],
        cost_estimate=pl.CostEstimate(flops=0, bytes_accessed=16_000_000, transcendentals=0),
        name="pack_tiles",
    )(slots, child_tiles)


def extend_kernel(id_ref, front_ref, arrived_ref, out_ref, panel_ref, acc_ref):
    cols_local = front_ref.shape[1] // TILE
    acc_ref[...] = front_ref[...].astype(jnp.float32)

    def add(s, carry):
        local = id_ref[s]

        @pl.when(local >= 0)
        def _():
            rows = pl.ds(pl.multiple_of(local // cols_local * TILE, TILE), TILE)
            cols = pl.ds(pl.multiple_of(local % cols_local * TILE, TILE), TILE)
            acc_ref[rows, cols] = acc_ref[rows, cols] + arrived_ref[s].astype(jnp.float32)

        return carry

    lax.fori_loop(0, arrived_ref.shape[0], add, 0)
    total = acc_ref[...].astype(jnp.bfloat16)
    out_ref[...] = total
    panel_ref[...] = total[2 * TILE :, 0:TILE]


def extend(ids, front, arrived):
    vm = pl.BlockSpec(memory_space=pltpu.VMEM)
    return pl.pallas_call(
        extend_kernel,
        out_shape=(
            jax.ShapeDtypeStruct(front.shape, jnp.bfloat16),
            jax.ShapeDtypeStruct((front.shape[0] - 2 * TILE, TILE), jnp.bfloat16),
        ),
        in_specs=[pl.BlockSpec(memory_space=pltpu.SMEM), vm, vm],
        out_specs=(vm, vm),
        scratch_shapes=[pltpu.VMEM(front.shape, jnp.float32)],
        compiler_params=pltpu.CompilerParams(vmem_limit_bytes=48 * 1024 * 1024),
        cost_estimate=pl.CostEstimate(flops=10_000_000, bytes_accessed=30_000_000, transcendentals=0),
        name="extend_add",
    )(ids, front, arrived)


def finish_kernel(place_ref, xh_ref, xl_ref, row_ref, col_ref, own_ref, assembled_ref, out_ref, a_ref, p_ref):
    step = pl.program_id(0)
    rows_low = row_ref.shape[1] * TILE
    cols_low = col_ref.shape[1] * TILE
    total = rows_low + cols_low
    c = place_ref[1]
    width = 2 * TILE

    @pl.when(step == 0)
    def _():
        out_ref[...] = assembled_ref[...].astype(jnp.float32)
        out_ref[0 : 2 * TILE, :] = jnp.zeros((2 * TILE, out_ref.shape[1]), jnp.float32)
        for a in range(2):
            out_ref[a * TILE : (a + 1) * TILE, 0:TILE] = own_ref[a].astype(jnp.float32)

    for s in range(PANEL // width):

        @pl.when(step == s)
        def _():
            for piece in range(2):
                lanes = slice(s * width + piece * TILE, s * width + (piece + 1) * TILE)
                a_ref[0:rows_low, lanes] = row_ref[piece].reshape(rows_low, TILE)
                a_ref[rows_low:total, lanes] = col_ref[piece].reshape(cols_low, TILE)
            depth = (s + 1) * width
            chunk = total // 6

            def solve(b, carry):
                rows = pl.ds(pl.multiple_of(b * chunk, chunk), chunk)
                a = a_ref[rows, 0:depth]
                p = jnp.dot(a, xh_ref[0:depth, :], preferred_element_type=jnp.float32) + jnp.dot(
                    a, xl_ref[0:depth, :], preferred_element_type=jnp.float32
                )
                p_ref[rows, :] = p.astype(jnp.bfloat16)
                return carry

            lax.fori_loop(0, 6, solve, 0)

    @pl.when(step == c // 2)
    def _():
        lane = pl.multiple_of(c % 2 * TILE, TILE)
        out_ref[2 * TILE :, 0:TILE] = p_ref[0:rows_low, pl.ds(lane, TILE)].astype(jnp.float32)

    def update(b, carry):
        rows = pl.ds(pl.multiple_of(b * 256, 256), 256)
        u = lax.dot_general(
            p_ref[rows, :], p_ref[rows_low:total, :], NT_DIMS, preferred_element_type=jnp.float32
        )
        target = pl.ds(pl.multiple_of(b * 256 + 2 * TILE, 256), 256)
        out_ref[target, TILE:] = out_ref[target, TILE:] - u
        return carry

    lax.fori_loop(0, rows_low // 256, update, 0)


def finish(place, xh, xl, row_raw, col_raw, own, assembled):
    width = 2 * TILE
    tiles_row = row_raw.shape[1]
    tiles_col = col_raw.shape[1]
    total = (tiles_row + tiles_col) * TILE
    vm = pl.BlockSpec(memory_space=pltpu.VMEM)
    return pl.pallas_call(
        finish_kernel,
        grid=(PANEL // width,),
        out_shape=jax.ShapeDtypeStruct(assembled.shape, jnp.float32),
        in_specs=[
            pl.BlockSpec(memory_space=pltpu.SMEM),
            pl.BlockSpec((PANEL, width), lambda s: (0, s)),
            pl.BlockSpec((PANEL, width), lambda s: (0, s)),
            pl.BlockSpec((2, tiles_row, TILE, TILE), lambda s: (s, 0, 0, 0)),
            pl.BlockSpec((2, tiles_col, TILE, TILE), lambda s: (s, 0, 0, 0)),
            vm,
            vm,
        ],
        out_specs=vm,
        scratch_shapes=[
            pltpu.VMEM((total, PANEL), jnp.bfloat16),
            pltpu.VMEM((total, width), jnp.bfloat16),
        ],
        compiler_params=pltpu.CompilerParams(
            vmem_limit_bytes=56 * 1024 * 1024, dimension_semantics=("arbitrary",)
        ),
        cost_estimate=pl.CostEstimate(flops=40_000_000_000, bytes_accessed=50_000_000, transcendentals=0),
        name="solve_update",
    )(place, xh, xl, row_raw, col_raw, own, assembled)


def per_device(front, child_tiles, tile_map):
    rows_local = front.shape[0]
    cols_local = front.shape[3]
    row_count = lax.axis_size("row")
    col_count = lax.axis_size("col")
    device_count = row_count * col_count
    row_index = lax.axis_index("row")
    col_index = lax.axis_index("col")
    both = ("row", "col")
    corner = front[0:2, 0, :, 0, 0, :]
    corner = lax.all_gather(corner, both, axis=0, tiled=False)

    owners = tile_map[:, 0] % row_count * col_count + tile_map[:, 1] % col_count
    local_ids = tile_map[:, 0] // row_count * cols_local + tile_map[:, 1] // col_count
    owner_hits = (owners[:, None] == jnp.arange(device_count)[None, :]).astype(jnp.int32)
    slot_rank = jnp.sum(jnp.cumsum(owner_hits, 0) * owner_hits, 1) - 1
    slot_index = owners * CAP + slot_rank
    packed = pack(slot_index, child_tiles)
    targets = jnp.full((device_count * CAP,), -1, jnp.int32).at[slot_index].set(local_ids)
    arrived = lax.all_to_all(
        packed.reshape(device_count, CAP, TILE, TILE), both, split_axis=0, concat_axis=0, tiled=True
    )
    arrived_ids = lax.all_to_all(
        targets.reshape(device_count, CAP), both, split_axis=0, concat_axis=0, tiled=True
    )

    place = jnp.stack([row_index, col_index]).astype(jnp.int32)
    own, xh, xl = factor_corner(corner, place)

    assembled, panel = extend(
        arrived_ids.reshape(device_count * CAP),
        front.reshape(rows_local * TILE, cols_local * TILE),
        arrived.reshape(device_count * CAP, TILE, TILE),
    )
    low_tiles = rows_local - 2
    panel = panel.reshape(low_tiles, TILE, TILE)
    row_raw = lax.all_gather(panel, "col", axis=0, tiled=False)
    split_panel = panel.reshape(low_tiles // 2, 2, TILE, TILE)
    halves = (split_panel[:, 0], split_panel[:, 1])
    parity = col_index % 2
    received = []
    for k in range(2):
        pairs = []
        for r in range(row_count):
            for c in range(col_count):
                h = (c % 2) ^ k
                pairs.append((r * col_count + c, (c // 2) * col_count + row_count * h + r))
        outgoing = jnp.where(parity == k, halves[0], halves[1])
        received.append(lax.ppermute(outgoing, both, pairs))
    high = col_index // row_count
    first = jnp.where(high == 0, received[0], received[1])
    second = jnp.where(high == 0, received[1], received[0])
    col_raw = lax.all_gather(jnp.stack([first, second]), "row", axis=0, tiled=True)
    out = finish(place, xh, xl, row_raw, col_raw, own, assembled)
    return out.reshape(rows_local, 1, TILE, cols_local, 1, TILE)


def solution(mesh):
    in_specs = (
        P(None, "row", None, None, "col", None),
        P(("row", "col"), None, None),
        P(("row", "col"), None),
    )
    out_specs = P(None, "row", None, None, "col", None)
    return jax.shard_map(
        per_device, mesh=mesh, in_specs=in_specs, out_specs=out_specs, check_vma=False
    )
```

```python
import functools
import numpy as np
import jax
import jax.numpy as jnp
from jax import lax
from jax.experimental import pallas as pl
from jax.experimental.pallas import tpu as pltpu
from jax.sharding import PartitionSpec as P

CAP = 2
PANEL = 2048
TILE = 128
NT_DIMS = (((1,), (1,)), ((), ()))


def split2(x):
    hi = x.astype(jnp.bfloat16)
    lo = (x - hi.astype(jnp.float32)).astype(jnp.bfloat16)
    return hi, lo


def nt(a, b):
    return lax.dot_general(a, b, NT_DIMS, preferred_element_type=jnp.float32)


def spread8(x):
    return jnp.broadcast_to(x, (8, TILE))


def total(terms):
    acc = terms[0]
    for term in terms[1:]:
        acc = acc + term
    return acc


def invert_tile(a_ref, i_ref, s_ref, out_ref, beside):
    row = lax.broadcasted_iota(jnp.int32, (TILE, TILE), 0)
    col = lax.broadcasted_iota(jnp.int32, (TILE, TILE), 1)
    i_ref[...] = (row == col).astype(jnp.float32)
    steps = TILE // 8
    for g in range(steps):
        base = 8 * g
        group = a_ref[base : base + 8, :]
        for k in range(8):
            s_ref[8 * k : 8 * k + 8, :] = spread8(group[:, base + k : base + k + 1])
        d = {}
        for k in range(8):
            for i in range(k, 8):
                d[i, k] = spread8(s_ref[8 * k + i : 8 * k + i + 1, :])
        ga = [spread8(a_ref[base + j : base + j + 1, :]) for j in range(8)]
        gi = [spread8(i_ref[base + j : base + j + 1, :]) for j in range(8)]
        rs = {}
        lo = {}
        for j in range(0, 8, 2):
            rs[j] = lax.rsqrt(d[j, j])
            det = lax.rsqrt(d[j, j] * d[j + 1, j + 1] - d[j + 1, j] * d[j + 1, j])
            rs[j + 1] = det * (d[j, j] * rs[j])
            lo[j + 1, j] = d[j + 1, j] * rs[j]
            for i in range(j + 2, 8):
                lo[i, j] = d[i, j] * rs[j]
                lo[i, j + 1] = (d[i, j + 1] - lo[i, j] * lo[j + 1, j]) * rs[j + 1]
            for k in range(j + 2, 8):
                for i in range(k, 8):
                    d[i, k] = d[i, k] - (lo[i, j] * lo[k, j] + lo[i, j + 1] * lo[k, j + 1])
        t = {}
        for j in range(8):
            t[j, j] = rs[j]
            for m in range(j):
                t[j, m] = -(total([lo[j, k] * t[k, m] for k in range(m, j)]) * rs[j])
        ui = [total([t[i, j] * gi[j] for j in range(i + 1)]) for i in range(8)]
        for i in range(8):
            out_ref[base + i : base + i + 1, :] = ui[i][0:1, :]
        if g < steps - 1:
            ua = [total([t[i, j] * ga[j] for j in range(i + 1)]) for i in range(8)]
            va = [total([t[i, j] * ua[i] for i in range(j, 8)]) for j in range(8)]
            vi = [total([t[i, j] * ui[i] for i in range(j, 8)]) for j in range(8)]
        for h in range(g + 1, steps):
            rows = slice(8 * h, 8 * h + 8)
            block = a_ref[rows, :]
            acc_a = block
            acc_i = i_ref[rows, :]
            for j in range(8):
                c = spread8(block[:, base + j : base + j + 1])
                acc_a = acc_a - c * va[j]
                acc_i = acc_i - c * vi[j]
            a_ref[rows, :] = acc_a
            i_ref[rows, :] = acc_i
        beside(g)


def unit_table(first, last):
    pairs = PANEL // 256
    count = pairs - first
    table = np.full((pairs + 1, 64), count * 8, np.int32)
    lengths = np.zeros((pairs + 1,), np.int32)
    for p in range(first, last + 1):
        units = []
        prev = p - 1
        start = p + 1 if p < last else p
        if prev >= first:
            for q in range(start, pairs):
                units += [(q - first) * 8 + b for b in range(pairs) if b <= prev or b >= q]
        lengths[p] = len(units)
        table[p, : len(units)] = units
    return np.concatenate([table.reshape(-1), lengths])


SLOTS = 64


def factor_kernel(first, last, place_ref, unit_ref, source_ref, own_ref, xh_ref, xl_ref, *rest):
    tiles = PANEL // TILE
    pairs = tiles // 2
    if last < pairs:
        next_ref, rest = rest[0], rest[1:]
    m_ref, eh_ref, el_ref, a_ref, o_ref, i_ref, s_ref, t_ref, sem = rest
    if first == 0:
        for j in range(tiles):
            for i in range(tiles):
                spot = (j // 2, slice(i * TILE, (i + 1) * TILE), slice(j % 2 * TILE, (j % 2 + 1) * TILE))
                if i >= j:
                    m_ref[spot] = source_ref[i % 8 * 16 + j, i // 8].astype(jnp.float32)
                else:
                    m_ref[spot] = jnp.zeros((TILE, TILE), jnp.float32)
    else:
        load = pltpu.make_async_copy(source_ref, m_ref.at[pl.ds(0, pairs - first)], sem)
        load.start()
        load.wait()
    own_ref[...] = jnp.zeros_like(own_ref)
    r = place_ref[0]
    c = place_ref[1]
    row = lax.broadcasted_iota(jnp.int32, (TILE, TILE), 0)
    col = lax.broadcasted_iota(jnp.int32, (TILE, TILE), 1)
    identity = (row == col).astype(jnp.float32)
    zero = jnp.zeros((TILE, TILE), jnp.bfloat16)

    def product(rows, cols, buf):
        lh, ll = eh_ref[buf, rows, :], el_ref[buf, rows, :]
        rh, rl = eh_ref[buf, cols, :], el_ref[buf, cols, :]
        return nt(lh, rh) + nt(lh, rl) + nt(ll, rh)

    def block_rows(b):
        return pl.ds(pl.multiple_of(b * 256, 256), 256)

    def tile_rows(i):
        return pl.ds(pl.multiple_of(i * TILE, TILE), TILE)

    def apply(code, buf):
        q = code // 8
        rows = block_rows(code % 8)
        cols = block_rows(jnp.minimum(q + first, pairs - 1))
        m_ref[q, rows, :] = m_ref[q, rows, :] - product(rows, cols, buf)

    def keep_own(k, buf, half):
        th, tl = split2(t_ref[...])
        oh, ol = split2(o_ref[...])
        both = jnp.concatenate([oh, ol], 1)
        diag = nt(both, jnp.concatenate([th, th], 1)) + nt(both, jnp.concatenate([tl, tl], 1))
        diag = jnp.where(row >= col, diag, 0.0).astype(jnp.bfloat16)

        @pl.when(k == c)
        def _():
            for a in range(2):
                i = r + a * 8
                src = eh_ref[buf, tile_rows(i), half * TILE : (half + 1) * TILE]
                own_ref[a] = jnp.where(i == k, diag, jnp.where(i > k, src, zero))

    def column(p, buf, half):
        th, tl = split2(t_ref[...])
        tt1 = jnp.concatenate([th, th], 1)
        tt2 = jnp.concatenate([tl, tl], 1)
        lanes = slice(half * TILE, (half + 1) * TILE)
        for b in range(pairs):
            rows = slice(b * 256, (b + 1) * 256)
            ch, cl = split2(m_ref[p - first, rows, lanes])
            both = jnp.concatenate([ch, cl], 1)
            eh, el = split2(nt(both, tt1) + nt(both, tt2))
            eh_ref[buf, rows, lanes] = eh
            el_ref[buf, rows, lanes] = el

    def step(p, carry):
        local = p - first
        buf = p % 2
        old = 1 - buf
        k = 2 * p
        m_ref[local, tile_rows(k), TILE:] = jnp.zeros((TILE, TILE), jnp.float32)

        diag = m_ref[local, tile_rows(k), 0:TILE]
        if first == 0:
            new = diag - product(tile_rows(k), tile_rows(k), old)
            diag = jnp.where(p > first, new, diag)
        else:
            new = diag - product(tile_rows(k), tile_rows(k), old)
            diag = jnp.where(p > first, new, diag)
        a_ref[...] = diag
        o_ref[...] = diag

        def first_beside(g):
            if g < 8:
                rows = slice(g * 256, (g + 1) * 256)
                old_block = m_ref[local, rows, :]
                new_block = old_block - product(rows, block_rows(p), old)
                m_ref[local, rows, :] = jnp.where(p > first, new_block, old_block)
            else:
                apply(unit_ref[p * SLOTS + g - 8], old)

        invert_tile(a_ref, i_ref, s_ref, t_ref, first_beside)
        m_ref[local, tile_rows(k), 0:TILE] = identity
        m_ref[local, tile_rows(k), TILE:] = jnp.zeros((TILE, TILE), jnp.float32)
        column(p, buf, 0)
        keep_own(k, buf, 0)

        def pair_product(rows):
            h = eh_ref[buf, rows, 0:TILE]
            l = el_ref[buf, rows, 0:TILE]
            fh = eh_ref[buf, tile_rows(k + 1), 0:TILE]
            fl = el_ref[buf, tile_rows(k + 1), 0:TILE]
            both = jnp.concatenate([h, l], 1)
            return nt(both, jnp.concatenate([fh, fh], 1)) + nt(both, jnp.concatenate([fl, fl], 1))

        diag = m_ref[local, tile_rows(k + 1), TILE:] - pair_product(tile_rows(k + 1))
        a_ref[...] = diag
        o_ref[...] = diag

        def second_beside(g):
            if g < 8:
                rows = slice(g * 256, (g + 1) * 256)
                m_ref[local, rows, TILE:] = m_ref[local, rows, TILE:] - pair_product(rows)
            apply(unit_ref[p * SLOTS + 8 + g], old)
            if g >= 12:
                apply(unit_ref[p * SLOTS + 12 + g], old)

        invert_tile(a_ref, i_ref, s_ref, t_ref, second_beside)
        m_ref[local, tile_rows(k + 1), TILE:] = identity
        column(p, buf, 1)
        keep_own(k + 1, buf, 1)
        eh_ref[buf, tile_rows(k + 1), 0:TILE] = zero
        el_ref[buf, tile_rows(k + 1), 0:TILE] = zero
        wide = pl.ds(pl.multiple_of(local * 256, 256), 256)
        depth = last * 256
        xh_ref[:, wide] = eh_ref[buf, 0:depth, :]
        xl_ref[:, wide] = el_ref[buf, 0:depth, :]
        return carry

    lax.fori_loop(first, last, step, 0)
    if last < pairs:
        def flush(u, carry):
            apply(unit_ref[last * SLOTS + u], (last - 1) % 2)
            return carry

        lax.fori_loop(0, unit_ref[(pairs + 1) * SLOTS + last], flush, 0)
        next_ref[...] = m_ref[last - first : pairs - first]


def factor_stage(first, last, place, source):
    pairs = PANEL // 256
    vm = pl.BlockSpec(memory_space=pltpu.VMEM)
    smem = pl.BlockSpec(memory_space=pltpu.SMEM)
    wide = (last - first) * 256
    out_shape = [
        jax.ShapeDtypeStruct((2, TILE, TILE), jnp.bfloat16),
        jax.ShapeDtypeStruct((last * 256, wide), jnp.bfloat16),
        jax.ShapeDtypeStruct((last * 256, wide), jnp.bfloat16),
    ]
    if last < pairs:
        out_shape.append(jax.ShapeDtypeStruct((pairs - last, PANEL, 256), jnp.float32))
    tile = pltpu.VMEM((TILE, TILE), jnp.float32)
    return pl.pallas_call(
        functools.partial(factor_kernel, first, last),
        out_shape=tuple(out_shape),
        in_specs=[smem, smem, vm if first == 0 else pl.BlockSpec(memory_space=pl.ANY)],
        out_specs=tuple(vm for _ in out_shape),
        scratch_shapes=[
            pltpu.VMEM((pairs - first + 1, PANEL, 256), jnp.float32),
            pltpu.VMEM((2, PANEL, 256), jnp.bfloat16),
            pltpu.VMEM((2, PANEL, 256), jnp.bfloat16),
            tile,
            tile,
            tile,
            tile,
            tile,
            pltpu.SemaphoreType.DMA,
        ],
        compiler_params=pltpu.CompilerParams(vmem_limit_bytes=60 * 1024 * 1024),
        cost_estimate=pl.CostEstimate(flops=60_000_000_000, bytes_accessed=24_000_000, transcendentals=0),
        name="factor_corner",
    )(place, jnp.asarray(unit_table(first, last)), source)


def pack_kernel(slot_ref, child_ref, first_ref, second_ref):
    def move(t, carry):
        slot = slot_ref[t]

        @pl.when(slot % CAP == 0)
        def _():
            first_ref[slot // CAP] = child_ref[t]

        @pl.when(slot % CAP == 1)
        def _():
            second_ref[slot // CAP] = child_ref[t]

        return carry

    lax.fori_loop(0, child_ref.shape[0], move, 0)


def pack(slots, child_tiles):
    count = child_tiles.shape[0]
    vm = pl.BlockSpec(memory_space=pltpu.VMEM)
    return pl.pallas_call(
        pack_kernel,
        out_shape=tuple(jax.ShapeDtypeStruct((count, TILE, TILE), jnp.bfloat16) for _ in range(CAP)),
        in_specs=[pl.BlockSpec(memory_space=pltpu.SMEM), vm],
        out_specs=(vm, vm),
        compiler_params=pltpu.CompilerParams(vmem_limit_bytes=32 * 1024 * 1024),
        cost_estimate=pl.CostEstimate(flops=0, bytes_accessed=16_000_000, transcendentals=0),
        name="pack_tiles",
    )(slots, child_tiles)


def extend_kernel(id_ref, front_ref, first_ref, second_ref, after_ref, out_ref, panel_ref, acc_ref):
    cols_local = front_ref.shape[1] // TILE
    acc_ref[...] = front_ref[...].astype(jnp.float32)

    def add(s, carry):
        for part, tile_ref in enumerate((first_ref, second_ref)):
            local = id_ref[CAP * s + part]

            @pl.when(local >= 0)
            def _():
                rows = pl.ds(pl.multiple_of(local // cols_local * TILE, TILE), TILE)
                cols = pl.ds(pl.multiple_of(local % cols_local * TILE, TILE), TILE)
                acc_ref[rows, cols] = acc_ref[rows, cols] + tile_ref[s].astype(jnp.float32)

        return carry

    lax.fori_loop(0, first_ref.shape[0], add, 0)
    summed = acc_ref[...].astype(jnp.bfloat16)
    out_ref[...] = summed
    panel_ref[...] = summed[2 * TILE :, 0:TILE]


def extend(ids, front, first, second, after):
    vm = pl.BlockSpec(memory_space=pltpu.VMEM)
    return pl.pallas_call(
        extend_kernel,
        out_shape=(
            jax.ShapeDtypeStruct(front.shape, jnp.bfloat16),
            jax.ShapeDtypeStruct((front.shape[0] - 2 * TILE, TILE), jnp.bfloat16),
        ),
        in_specs=[pl.BlockSpec(memory_space=pltpu.SMEM), vm, vm, vm, pl.BlockSpec(memory_space=pl.ANY)],
        out_specs=(vm, vm),
        scratch_shapes=[pltpu.VMEM(front.shape, jnp.float32)],
        compiler_params=pltpu.CompilerParams(vmem_limit_bytes=48 * 1024 * 1024),
        cost_estimate=pl.CostEstimate(flops=10_000_000, bytes_accessed=30_000_000, transcendentals=0),
        name="extend_add",
    )(ids, front, first, second, after)


def finish_kernel(
    place_ref, xh1_ref, xl1_ref, xh2_ref, xl2_ref, row_ref, col_ref, own1_ref, own2_ref, assembled_ref, out_ref, a_ref, p_ref, acc_ref
):
    step = pl.program_id(0)
    steps = PANEL // (2 * TILE)
    rows_low = row_ref.shape[1] * TILE
    cols_low = col_ref.shape[1] * TILE
    total = rows_low + cols_low
    cols_local = assembled_ref.shape[1] // TILE
    c = place_ref[1]
    width = 2 * TILE

    @pl.when(step == 0)
    def _():
        top = 2 * TILE * cols_local
        out_ref[0:top, :] = jnp.zeros((top, TILE), jnp.float32)
        for a in range(2):
            rows = pl.ds(a * TILE * cols_local, TILE, stride=cols_local)
            out_ref[rows, :] = own1_ref[a].astype(jnp.float32) + own2_ref[a].astype(jnp.float32)
        acc_ref[...] = assembled_ref[2 * TILE :, TILE:].astype(jnp.float32)

    for s in range(steps):

        @pl.when(step == s)
        def _():
            for piece in range(2):
                lanes = slice(s * width + piece * TILE, s * width + (piece + 1) * TILE)
                a_ref[0:rows_low, lanes] = row_ref[piece].reshape(rows_low, TILE)
                a_ref[rows_low:total, lanes] = col_ref[piece].reshape(cols_low, TILE)
            depth = (s + 1) * width
            chunk = total
            xh_ref, xl_ref = (xh1_ref, xl1_ref) if s < steps // 2 else (xh2_ref, xl2_ref)

            def solve(b, carry):
                rows = pl.ds(pl.multiple_of(b * chunk, chunk), chunk)
                a = a_ref[rows, 0:depth]
                p = jnp.dot(a, xh_ref[0:depth, :], preferred_element_type=jnp.float32) + jnp.dot(
                    a, xl_ref[0:depth, :], preferred_element_type=jnp.float32
                )
                p_ref[rows, :] = p.astype(jnp.bfloat16)
                return carry

            lax.fori_loop(0, 1, solve, 0)

    @pl.when(step == c // 2)
    def _():
        lane = pl.multiple_of(c % 2 * TILE, TILE)
        rows = pl.ds(2 * TILE * cols_local, rows_low, stride=cols_local)
        out_ref[rows, :] = p_ref[0:rows_low, pl.ds(lane, TILE)].astype(jnp.float32)

    def update(b):
        rows = pl.ds(pl.multiple_of(b * 1792, 1792), 1792)
        return acc_ref[rows, :] - nt(p_ref[rows, :], p_ref[rows_low:total, :])

    def keep(b, carry):
        acc_ref[pl.ds(pl.multiple_of(b * 1792, 1792), 1792), :] = update(b)
        return carry

    def write(b, carry):
        u = update(b)
        for t in range(1, cols_local):
            target = pl.ds((b * 1792 + 2 * TILE) * cols_local + t, 1792, stride=cols_local)
            out_ref[target, :] = u[:, (t - 1) * TILE : t * TILE]
        return carry

    @pl.when(step < steps - 1)
    def _():
        lax.fori_loop(0, rows_low // 1792, keep, 0)

    @pl.when(step == steps - 1)
    def _():
        lax.fori_loop(0, rows_low // 1792, write, 0)


def finish(place, x1, x2, row_raw, col_raw, own1, own2, assembled):
    width = 2 * TILE
    steps = PANEL // width
    mid = steps // 2
    tiles_row = row_raw.shape[1]
    tiles_col = col_raw.shape[1]
    total = (tiles_row + tiles_col) * TILE
    vm = pl.BlockSpec(memory_space=pltpu.VMEM)
    early = pl.BlockSpec((PANEL // 2, width), lambda s: (0, jnp.minimum(s, mid - 1)))
    late = pl.BlockSpec((PANEL, width), lambda s: (0, jnp.maximum(s - mid, 0)))
    return pl.pallas_call(
        finish_kernel,
        grid=(steps,),
        out_shape=jax.ShapeDtypeStruct((assembled.shape[0] * assembled.shape[1] // TILE, TILE), jnp.float32),
        in_specs=[
            pl.BlockSpec(memory_space=pltpu.SMEM),
            early,
            early,
            late,
            late,
            pl.BlockSpec((2, tiles_row, TILE, TILE), lambda s: (s, 0, 0, 0)),
            pl.BlockSpec((2, tiles_col, TILE, TILE), lambda s: (s, 0, 0, 0)),
            vm,
            vm,
            vm,
        ],
        out_specs=vm,
        scratch_shapes=[
            pltpu.VMEM((total, PANEL), jnp.bfloat16),
            pltpu.VMEM((total, width), jnp.bfloat16),
            pltpu.VMEM((tiles_row * TILE, tiles_col * TILE), jnp.float32),
        ],
        compiler_params=pltpu.CompilerParams(
            vmem_limit_bytes=56 * 1024 * 1024, dimension_semantics=("arbitrary",)
        ),
        cost_estimate=pl.CostEstimate(flops=40_000_000_000, bytes_accessed=50_000_000, transcendentals=0),
        name="solve_update",
    )(place, *x1, *x2, row_raw, col_raw, own1, own2, assembled)


def per_device(front, child_tiles, tile_map):
    rows_local = front.shape[0]
    cols_local = front.shape[3]
    row_count = lax.axis_size("row")
    col_count = lax.axis_size("col")
    device_count = row_count * col_count
    row_index = lax.axis_index("row")
    col_index = lax.axis_index("col")
    both = ("row", "col")
    corner = front[0:2, 0, :, 0, 0, :]
    corner = lax.all_gather(corner, both, axis=0, tiled=False)

    owners = tile_map[:, 0] % row_count * col_count + tile_map[:, 1] % col_count
    local_ids = tile_map[:, 0] // row_count * cols_local + tile_map[:, 1] // col_count
    owner_hits = (owners[:, None] == jnp.arange(device_count)[None, :]).astype(jnp.int32)
    slot_rank = jnp.sum(jnp.cumsum(owner_hits, 0) * owner_hits, 1) - 1
    slot_index = owners * CAP + slot_rank
    def exchange(x):
        return lax.all_to_all(x, both, split_axis=0, concat_axis=0, tiled=True)

    first, second = pack(slot_index, child_tiles)
    targets = jnp.full((device_count * CAP,), -1, jnp.int32).at[slot_index].set(local_ids)
    arrived_ids = exchange(targets.reshape(device_count, CAP))
    first = exchange(first)
    flat_front = front.reshape(rows_local * TILE, cols_local * TILE)
    corner, second, flat_front = lax.optimization_barrier((corner, second, flat_front))
    second = exchange(second)

    place = jnp.stack([row_index, col_index]).astype(jnp.int32)
    own1, xh1, xl1, state = factor_stage(0, 4, place, corner)
    assembled, panel = extend(arrived_ids.reshape(device_count * CAP), flat_front, first, second, own1)
    low_tiles = rows_local - 2
    panel = panel.reshape(low_tiles, TILE, TILE)
    row_raw = lax.all_gather(panel, "col", axis=0, tiled=False)
    split_panel = panel.reshape(low_tiles // 2, 2, TILE, TILE)
    halves = (split_panel[:, 0], split_panel[:, 1])
    parity = col_index % 2
    received = []
    for k in range(2):
        pairs = []
        for r in range(row_count):
            for c in range(col_count):
                h = (c % 2) ^ k
                pairs.append((r * col_count + c, (c // 2) * col_count + row_count * h + r))
        outgoing = jnp.where(parity == k, halves[0], halves[1])
        received.append(lax.ppermute(outgoing, both, pairs))
    high = col_index // row_count
    first = jnp.where(high == 0, received[0], received[1])
    second = jnp.where(high == 0, received[1], received[0])
    pieces = jnp.broadcast_to(jnp.stack([first, second]), (row_count, 2) + first.shape)
    state, pieces = lax.optimization_barrier((state, pieces))
    col_raw = lax.all_to_all(
        pieces, "row", split_axis=0, concat_axis=0, tiled=True
    ).reshape(col_count, low_tiles // 2, TILE, TILE)
    own2, xh2, xl2 = factor_stage(4, 8, place, state)
    out = finish(place, (xh1, xl1), (xh2, xl2), row_raw, col_raw, own1, own2, assembled)
    return out.reshape(rows_local, 1, TILE, cols_local, 1, TILE)


def solution(mesh):
    in_specs = (
        P(None, "row", None, None, "col", None),
        P(("row", "col"), None, None),
        P(("row", "col"), None),
    )
    out_specs = P(None, "row", None, None, "col", None)
    return jax.shard_map(
        per_device, mesh=mesh, in_specs=in_specs, out_specs=out_specs, check_vma=False
    )
```

```python
import functools
import numpy as np
import jax
import jax.numpy as jnp
from jax import lax
from jax.experimental import pallas as pl
from jax.experimental.pallas import tpu as pltpu
from jax.sharding import PartitionSpec as P

CAP = 2
SPLIT = 2
PANEL = 2048
TILE = 128
NT_DIMS = (((1,), (1,)), ((), ()))
SLOTS = 32


def split2(x):
    hi = x.astype(jnp.bfloat16)
    lo = (x - hi.astype(jnp.float32)).astype(jnp.bfloat16)
    return hi, lo


def nt(a, b):
    return lax.dot_general(a, b, NT_DIMS, preferred_element_type=jnp.float32)


def spread8(x):
    return jnp.broadcast_to(x, (8, TILE))


def total(terms):
    acc = terms[0]
    for term in terms[1:]:
        acc = acc + term
    return acc


def invert_tile(a_ref, i_ref, s_ref, out_ref, beside):
    row = lax.broadcasted_iota(jnp.int32, (TILE, TILE), 0)
    col = lax.broadcasted_iota(jnp.int32, (TILE, TILE), 1)
    i_ref[...] = (row == col).astype(jnp.float32)
    steps = TILE // 8
    for g in range(steps):
        base = 8 * g
        group = a_ref[base : base + 8, :]
        for k in range(8):
            s_ref[8 * k : 8 * k + 8, :] = spread8(group[:, base + k : base + k + 1])
        d = {}
        for k in range(8):
            for i in range(k, 8):
                d[i, k] = spread8(s_ref[8 * k + i : 8 * k + i + 1, :])
        ga = [spread8(a_ref[base + j : base + j + 1, :]) for j in range(8)]
        gi = [spread8(i_ref[base + j : base + j + 1, :]) for j in range(8)]
        rs = {}
        lo = {}
        for j in range(0, 8, 2):
            rs[j] = lax.rsqrt(d[j, j])
            det = lax.rsqrt(d[j, j] * d[j + 1, j + 1] - d[j + 1, j] * d[j + 1, j])
            rs[j + 1] = det * (d[j, j] * rs[j])
            lo[j + 1, j] = d[j + 1, j] * rs[j]
            for i in range(j + 2, 8):
                lo[i, j] = d[i, j] * rs[j]
                lo[i, j + 1] = (d[i, j + 1] - lo[i, j] * lo[j + 1, j]) * rs[j + 1]
            for k in range(j + 2, 8):
                for i in range(k, 8):
                    d[i, k] = d[i, k] - (lo[i, j] * lo[k, j] + lo[i, j + 1] * lo[k, j + 1])
        t = {}
        for j in range(8):
            t[j, j] = rs[j]
            for m in range(j):
                t[j, m] = -(total([lo[j, k] * t[k, m] for k in range(m, j)]) * rs[j])
        ui = [total([t[i, j] * gi[j] for j in range(i + 1)]) for i in range(8)]
        for i in range(8):
            out_ref[base + i : base + i + 1, :] = ui[i][0:1, :]
        if g < steps - 1:
            ua = [total([t[i, j] * ga[j] for j in range(i + 1)]) for i in range(8)]
            va = [total([t[i, j] * ua[i] for i in range(j, 8)]) for j in range(8)]
            vi = [total([t[i, j] * ui[i] for i in range(j, 8)]) for j in range(8)]
        for h in range(g + 1, steps):
            rows = slice(8 * h, 8 * h + 8)
            block = a_ref[rows, :]
            acc_a = block
            acc_i = i_ref[rows, :]
            for j in range(8):
                c = spread8(block[:, base + j : base + j + 1])
                acc_a = acc_a - c * va[j]
                acc_i = acc_i - c * vi[j]
            a_ref[rows, :] = acc_a
            i_ref[rows, :] = acc_i
        beside(g)


def unit_table(first, last):
    pairs = PANEL // 256
    table = np.full((pairs, SLOTS), (pairs - first) * 8, np.int32)
    for p in range(max(first, 1), last):
        units = [(q - first) * 8 + b for q in range(p + 1, pairs) for b in range(pairs) if b <= p - 1 or b >= q]
        table[p, : len(units)] = units
    return table.reshape(-1)


def factor_kernel(first, last, place_ref, unit_ref, *rest):
    tiles = PANEL // TILE
    pairs = tiles // 2
    if first == 0:
        source_ref, rest = rest[0], rest[1:]
    else:
        source_ref, oldh_ref, oldl_ref = rest[:3]
        rest = rest[3:]
    own_ref, xh_ref, xl_ref = rest[:3]
    rest = rest[3:]
    if last < pairs:
        next_ref, nexth_ref, nextl_ref = rest[:3]
        rest = rest[3:]
    m_ref, eh_ref, el_ref, a_ref, o_ref, i_ref, s_ref, t_ref, sem = rest
    if first == 0:
        for j in range(tiles):
            for i in range(tiles):
                spot = (j // 2, slice(i * TILE, (i + 1) * TILE), slice(j % 2 * TILE, (j % 2 + 1) * TILE))
                if i >= j:
                    m_ref[spot] = source_ref[i % 8 * 16 + j, i // 8].astype(jnp.float32)
                else:
                    m_ref[spot] = jnp.zeros((TILE, TILE), jnp.float32)
    else:
        loads = (
            pltpu.make_async_copy(source_ref, m_ref.at[pl.ds(0, pairs - first)], sem.at[0]),
            pltpu.make_async_copy(oldh_ref, eh_ref.at[(first - 1) % 2], sem.at[1]),
            pltpu.make_async_copy(oldl_ref, el_ref.at[(first - 1) % 2], sem.at[2]),
        )
        for load in loads:
            load.start()
        for load in loads:
            load.wait()
    own_ref[...] = jnp.zeros_like(own_ref)
    r = place_ref[0]
    c = place_ref[1]
    row = lax.broadcasted_iota(jnp.int32, (TILE, TILE), 0)
    col = lax.broadcasted_iota(jnp.int32, (TILE, TILE), 1)
    identity = (row == col).astype(jnp.float32)
    zero = jnp.zeros((TILE, TILE), jnp.bfloat16)

    def product(rows, cols, buf):
        lh, ll = eh_ref[buf, rows, :], el_ref[buf, rows, :]
        rh, rl = eh_ref[buf, cols, :], el_ref[buf, cols, :]
        return nt(lh, rh) + nt(lh, rl) + nt(ll, rh)

    def block_rows(b):
        return pl.ds(pl.multiple_of(b * 256, 256), 256)

    def tile_rows(i):
        return pl.ds(pl.multiple_of(i * TILE, TILE), TILE)

    def apply(code, buf):
        q = code // 8
        rows = block_rows(code % 8)
        cols = block_rows(jnp.minimum(q + first, pairs - 1))
        m_ref[q, rows, :] = m_ref[q, rows, :] - product(rows, cols, buf)

    def times(x, y):
        xh, xl = x
        yh, yl = y
        parts = nt(
            jnp.concatenate([xh, xl], 1),
            jnp.concatenate([jnp.concatenate([yh, yh], 1), jnp.concatenate([yl, yl], 1)], 0),
        )
        return parts[:, :TILE] + parts[:, TILE:]

    def keep_own(k, buf, half):
        @pl.when(k == c)
        def _():
            diag = times(split2(o_ref[...]), split2(t_ref[...]))
            diag = jnp.where(row >= col, diag, 0.0).astype(jnp.bfloat16)
            for a in range(2):
                i = r + a * 8
                src = eh_ref[buf, tile_rows(i), half * TILE : (half + 1) * TILE]
                own_ref[a] = jnp.where(i == k, diag, jnp.where(i > k, src, zero))

    def column(p, buf, half):
        inverse = split2(t_ref[...])
        lanes = slice(half * TILE, (half + 1) * TILE)
        for b in range(pairs):
            rows = slice(b * 256, (b + 1) * 256)
            eh, el = split2(times(split2(m_ref[p - first, rows, lanes]), inverse))
            eh_ref[buf, rows, lanes] = eh
            el_ref[buf, rows, lanes] = el

    def step(p, carry):
        local = p - first
        buf = p % 2
        old = 1 - buf
        k = 2 * p
        m_ref[local, tile_rows(k), TILE:] = jnp.zeros((TILE, TILE), jnp.float32)

        diag = m_ref[local, tile_rows(k), 0:TILE]
        diag = jnp.where(p > 0, diag - product(tile_rows(k), tile_rows(k), old), diag)
        a_ref[...] = diag
        o_ref[...] = diag

        def first_beside(g):
            if g < 8:
                rows = slice(g * 256, (g + 1) * 256)
                old_block = m_ref[local, rows, :]
                new_block = old_block - product(rows, block_rows(p), old)
                m_ref[local, rows, :] = jnp.where(p > 0, new_block, old_block)
            else:
                apply(unit_ref[p * SLOTS + g - 8], old)

        invert_tile(a_ref, i_ref, s_ref, t_ref, first_beside)
        m_ref[local, tile_rows(k), 0:TILE] = identity
        m_ref[local, tile_rows(k), TILE:] = jnp.zeros((TILE, TILE), jnp.float32)
        column(p, buf, 0)
        keep_own(k, buf, 0)

        def pair_product(rows):
            lanes = slice(0, TILE)
            return times(
                (eh_ref[buf, rows, lanes], el_ref[buf, rows, lanes]),
                (eh_ref[buf, tile_rows(k + 1), lanes], el_ref[buf, tile_rows(k + 1), lanes]),
            )

        diag = m_ref[local, tile_rows(k + 1), TILE:] - pair_product(tile_rows(k + 1))
        a_ref[...] = diag
        o_ref[...] = diag

        def second_beside(g):
            if g < 8:
                rows = slice(g * 256, (g + 1) * 256)
                m_ref[local, rows, TILE:] = m_ref[local, rows, TILE:] - pair_product(rows)
            apply(unit_ref[p * SLOTS + 8 + g], old)
            if g >= 12:
                apply(unit_ref[p * SLOTS + 12 + g], old)

        invert_tile(a_ref, i_ref, s_ref, t_ref, second_beside)
        m_ref[local, tile_rows(k + 1), TILE:] = identity
        column(p, buf, 1)
        keep_own(k + 1, buf, 1)
        eh_ref[buf, tile_rows(k + 1), 0:TILE] = zero
        el_ref[buf, tile_rows(k + 1), 0:TILE] = zero
        wide = pl.ds(pl.multiple_of(local * 256, 256), 256)
        depth = last * 256
        xh_ref[:, wide] = eh_ref[buf, 0:depth, :]
        xl_ref[:, wide] = el_ref[buf, 0:depth, :]
        return carry

    lax.fori_loop(first, last, step, 0)
    if last < pairs:
        next_ref[...] = m_ref[last - first : pairs - first]
        nexth_ref[...] = eh_ref[(last - 1) % 2]
        nextl_ref[...] = el_ref[(last - 1) % 2]


def factor_stage(first, last, place, *sources):
    pairs = PANEL // 256
    vm = pl.BlockSpec(memory_space=pltpu.VMEM)
    smem = pl.BlockSpec(memory_space=pltpu.SMEM)
    wide = (last - first) * 256
    out_shape = [
        jax.ShapeDtypeStruct((2, TILE, TILE), jnp.bfloat16),
        jax.ShapeDtypeStruct((last * 256, wide), jnp.bfloat16),
        jax.ShapeDtypeStruct((last * 256, wide), jnp.bfloat16),
    ]
    if last < pairs:
        out_shape.append(jax.ShapeDtypeStruct((pairs - last, PANEL, 256), jnp.float32))
        out_shape += [jax.ShapeDtypeStruct((PANEL, 256), jnp.bfloat16)] * 2
    tile = pltpu.VMEM((TILE, TILE), jnp.float32)
    return pl.pallas_call(
        functools.partial(factor_kernel, first, last),
        out_shape=tuple(out_shape),
        in_specs=[smem, smem] + ([vm] if first == 0 else [pl.BlockSpec(memory_space=pl.ANY)] * 3),
        out_specs=tuple(vm for _ in out_shape),
        scratch_shapes=[
            pltpu.VMEM((pairs - first + 1, PANEL, 256), jnp.float32),
            pltpu.VMEM((2, PANEL, 256), jnp.bfloat16),
            pltpu.VMEM((2, PANEL, 256), jnp.bfloat16),
            tile,
            tile,
            tile,
            tile,
            tile,
            pltpu.SemaphoreType.DMA((3,)),
        ],
        compiler_params=pltpu.CompilerParams(vmem_limit_bytes=60 * 1024 * 1024),
        cost_estimate=pl.CostEstimate(flops=60_000_000_000, bytes_accessed=24_000_000, transcendentals=0),
        name="factor_corner",
    )(place, jnp.asarray(unit_table(first, last)), *sources)


def pack_kernel(slot_ref, child_ref, packed_ref):
    def move(t, carry):
        packed_ref[slot_ref[t]] = child_ref[t]
        return carry

    lax.fori_loop(0, child_ref.shape[0], move, 0)


def pack(slots, child_tiles):
    count = child_tiles.shape[0]
    vm = pl.BlockSpec(memory_space=pltpu.VMEM)
    return pl.pallas_call(
        pack_kernel,
        out_shape=jax.ShapeDtypeStruct((CAP * count, TILE, TILE), jnp.bfloat16),
        in_specs=[pl.BlockSpec(memory_space=pltpu.SMEM), vm],
        out_specs=vm,
        compiler_params=pltpu.CompilerParams(vmem_limit_bytes=32 * 1024 * 1024),
        cost_estimate=pl.CostEstimate(flops=0, bytes_accessed=16_000_000, transcendentals=0),
        name="pack_tiles",
    )(slots, child_tiles)


def extend_kernel(id_ref, front_ref, arrived_ref, out_ref, panel_ref, acc_ref):
    cols_local = front_ref.shape[1] // TILE
    acc_ref[...] = front_ref[...].astype(jnp.float32)

    def add(s, carry):
        local = id_ref[s]

        @pl.when(local >= 0)
        def _():
            rows = pl.ds(pl.multiple_of(local // cols_local * TILE, TILE), TILE)
            cols = pl.ds(pl.multiple_of(local % cols_local * TILE, TILE), TILE)
            acc_ref[rows, cols] = acc_ref[rows, cols] + arrived_ref[s].astype(jnp.float32)

        return carry

    lax.fori_loop(0, arrived_ref.shape[0], add, 0)
    summed = acc_ref[...].astype(jnp.bfloat16)
    out_ref[...] = summed
    panel_ref[...] = summed[2 * TILE :, 0:TILE]


def extend(ids, front, arrived):
    vm = pl.BlockSpec(memory_space=pltpu.VMEM)
    return pl.pallas_call(
        extend_kernel,
        out_shape=(
            jax.ShapeDtypeStruct(front.shape, jnp.bfloat16),
            jax.ShapeDtypeStruct((front.shape[0] - 2 * TILE, TILE), jnp.bfloat16),
        ),
        in_specs=[pl.BlockSpec(memory_space=pltpu.SMEM), vm, vm],
        out_specs=(vm, vm),
        scratch_shapes=[pltpu.VMEM(front.shape, jnp.float32)],
        compiler_params=pltpu.CompilerParams(vmem_limit_bytes=48 * 1024 * 1024),
        cost_estimate=pl.CostEstimate(flops=10_000_000, bytes_accessed=30_000_000, transcendentals=0),
        name="extend_add",
    )(ids, front, arrived)


def finish_kernel(
    place_ref, xh1_ref, xl1_ref, xh2_ref, xl2_ref, row_ref, col_ref, own1_ref, own2_ref, assembled_ref, out_ref, a_ref, p_ref, sum_ref, acc_ref
):
    step = pl.program_id(0)
    steps = PANEL // (2 * TILE)
    rows_low = row_ref.shape[1] * TILE
    cols_low = col_ref.shape[1] * TILE
    total = rows_low + cols_low
    cols_local = assembled_ref.shape[1] // TILE
    c = place_ref[1]
    width = 2 * TILE

    @pl.when(step == 0)
    def _():
        top = 2 * TILE * cols_local
        out_ref[0:top, :] = jnp.zeros((top, TILE), jnp.float32)
        for a in range(2):
            rows = pl.ds(a * TILE * cols_local, TILE, stride=cols_local)
            out_ref[rows, :] = own1_ref[a].astype(jnp.float32) + own2_ref[a].astype(jnp.float32)
        acc_ref[...] = assembled_ref[2 * TILE :, TILE:].astype(jnp.float32)

    for piece in range(2):
        lanes = slice(piece * TILE, (piece + 1) * TILE)
        a_ref[step, 0:rows_low, lanes] = row_ref[piece].reshape(rows_low, TILE)
        a_ref[step, rows_low:total, lanes] = col_ref[piece].reshape(cols_low, TILE)

    def solve_with(xh_ref, xl_ref):
        def part(kk):
            rows = pl.ds(pl.multiple_of(kk * width, width), width)
            a = a_ref[kk]
            return jnp.dot(a, xh_ref[rows, :], preferred_element_type=jnp.float32) + jnp.dot(
                a, xl_ref[rows, :], preferred_element_type=jnp.float32
            )

        def solve(kk, carry):
            sum_ref[...] = sum_ref[...] + part(kk)
            return carry

        sum_ref[...] = jnp.zeros_like(sum_ref)
        lax.fori_loop(0, step, solve, 0)
        p_ref[...] = (sum_ref[...] + part(step)).astype(jnp.bfloat16)

    mid = xh1_ref.shape[0] // width

    @pl.when(step < mid)
    def _():
        solve_with(xh1_ref, xl1_ref)

    @pl.when(step >= mid)
    def _():
        solve_with(xh2_ref, xl2_ref)

    @pl.when(step == c // 2)
    def _():
        lane = pl.multiple_of(c % 2 * TILE, TILE)
        rows = pl.ds(2 * TILE * cols_local, rows_low, stride=cols_local)
        out_ref[rows, :] = p_ref[0:rows_low, pl.ds(lane, TILE)].astype(jnp.float32)

    def update(b, carry):
        rows = pl.ds(pl.multiple_of(b * chunk, chunk), chunk)
        acc_ref[rows, :] = acc_ref[rows, :] - nt(p_ref[rows, :], p_ref[rows_low:total, :])
        return carry

    chunk = rows_low
    lax.fori_loop(0, 1, update, 0)

    @pl.when(step == steps - 1)
    def _():
        def write(t, carry):
            lanes = pl.ds(pl.multiple_of((t - 1) * TILE, TILE), TILE)
            out_ref[pl.ds(2 * TILE * cols_local + t, rows_low, stride=cols_local), :] = acc_ref[:, lanes]
            return carry

        lax.fori_loop(1, cols_local, write, 0)


def finish(place, x1, x2, row_raw, col_raw, own1, own2, assembled):
    width = 2 * TILE
    steps = PANEL // width
    mid = x1[0].shape[1] // width
    tiles_row = row_raw.shape[1]
    tiles_col = col_raw.shape[1]
    total = (tiles_row + tiles_col) * TILE
    vm = pl.BlockSpec(memory_space=pltpu.VMEM)
    early = pl.BlockSpec((mid * width, width), lambda s: (0, jnp.minimum(s, mid - 1)))
    late = pl.BlockSpec((PANEL, width), lambda s: (0, jnp.maximum(s - mid, 0)))
    return pl.pallas_call(
        finish_kernel,
        grid=(steps,),
        out_shape=jax.ShapeDtypeStruct((assembled.shape[0] * assembled.shape[1] // TILE, TILE), jnp.float32),
        in_specs=[
            pl.BlockSpec(memory_space=pltpu.SMEM),
            early,
            early,
            late,
            late,
            pl.BlockSpec((2, tiles_row, TILE, TILE), lambda s: (s, 0, 0, 0)),
            pl.BlockSpec((2, tiles_col, TILE, TILE), lambda s: (s, 0, 0, 0)),
            vm,
            vm,
            vm,
        ],
        out_specs=vm,
        scratch_shapes=[
            pltpu.VMEM((steps, total, width), jnp.bfloat16),
            pltpu.VMEM((total, width), jnp.bfloat16),
            pltpu.VMEM((total, width), jnp.float32),
            pltpu.VMEM((tiles_row * TILE, tiles_col * TILE), jnp.float32),
        ],
        compiler_params=pltpu.CompilerParams(
            vmem_limit_bytes=56 * 1024 * 1024, dimension_semantics=("arbitrary",)
        ),
        cost_estimate=pl.CostEstimate(flops=40_000_000_000, bytes_accessed=50_000_000, transcendentals=0),
        name="solve_update",
    )(place, *x1, *x2, row_raw, col_raw, own1, own2, assembled)


def per_device(front, child_tiles, tile_map):
    rows_local = front.shape[0]
    cols_local = front.shape[3]
    row_count = lax.axis_size("row")
    col_count = lax.axis_size("col")
    device_count = row_count * col_count
    row_index = lax.axis_index("row")
    col_index = lax.axis_index("col")
    both = ("row", "col")
    corner = front[0:2, 0, :, 0, 0, :]
    corner = lax.all_gather(corner, both, axis=0, tiled=False)

    owners = tile_map[:, 0] % row_count * col_count + tile_map[:, 1] % col_count
    local_ids = tile_map[:, 0] // row_count * cols_local + tile_map[:, 1] // col_count
    owner_hits = (owners[:, None] == jnp.arange(device_count)[None, :]).astype(jnp.int32)
    slot_rank = jnp.sum(jnp.cumsum(owner_hits, 0) * owner_hits, 1) - 1
    slot_index = owners * CAP + slot_rank

    def exchange(x):
        return lax.all_to_all(
            x.reshape((device_count, CAP) + x.shape[1:]), both, split_axis=0, concat_axis=0, tiled=True
        ).reshape(x.shape)

    targets = jnp.full((device_count * CAP,), -1, jnp.int32).at[slot_index].set(local_ids)
    arrived = exchange(pack(slot_index, child_tiles))
    flat_front = front.reshape(rows_local * TILE, cols_local * TILE)
    targets, flat_front = lax.optimization_barrier((targets, flat_front))
    assembled, panel = extend(exchange(targets), flat_front, arrived)
    corner, panel = lax.optimization_barrier((corner, panel))

    place = jnp.stack([row_index, col_index]).astype(jnp.int32)
    own1, xh1, xl1, *state = factor_stage(0, SPLIT, place, corner)
    low_tiles = rows_local - 2
    panel = panel.reshape(low_tiles, TILE, TILE)
    row_raw = lax.all_gather(panel, "col", axis=0, tiled=False)
    split_panel = panel.reshape(low_tiles // 2, 2, TILE, TILE)
    halves = (split_panel[:, 0], split_panel[:, 1])
    parity = col_index % 2
    received = []
    for k in range(2):
        pairs = []
        for r in range(row_count):
            for c in range(col_count):
                h = (c % 2) ^ k
                pairs.append((r * col_count + c, (c // 2) * col_count + row_count * h + r))
        outgoing = jnp.where(parity == k, halves[0], halves[1])
        received.append(lax.ppermute(outgoing, both, pairs))
    high = col_index // row_count
    first = jnp.where(high == 0, received[0], received[1])
    second = jnp.where(high == 0, received[1], received[0])
    pieces = jnp.broadcast_to(jnp.stack([first, second]), (row_count, 2) + first.shape)
    *state, pieces = lax.optimization_barrier((*state, pieces))
    col_raw = lax.all_to_all(
        pieces, "row", split_axis=0, concat_axis=0, tiled=True
    ).reshape(col_count, low_tiles // 2, TILE, TILE)
    own2, xh2, xl2 = factor_stage(SPLIT, PANEL // 256, place, *state)
    out = finish(place, (xh1, xl1), (xh2, xl2), row_raw, col_raw, own1, own2, assembled)
    return out.reshape(rows_local, 1, TILE, cols_local, 1, TILE)


def solution(mesh):
    in_specs = (
        P(None, "row", None, None, "col", None),
        P(("row", "col"), None, None),
        P(("row", "col"), None),
    )
    out_specs = P(None, "row", None, None, "col", None)
    return jax.shard_map(
        per_device, mesh=mesh, in_specs=in_specs, out_specs=out_specs, check_vma=False
    )
```

```python
import functools
import numpy as np
import jax
import jax.numpy as jnp
from jax import lax
from jax.experimental import pallas as pl
from jax.experimental.pallas import tpu as pltpu
from jax.sharding import PartitionSpec as P

CAP = 2
HEAD = 16
SPLIT = 2
PANEL = 2048
TILE = 128
NT_DIMS = (((1,), (1,)), ((), ()))
SLOTS = 32


def split2(x):
    hi = x.astype(jnp.bfloat16)
    lo = (x - hi.astype(jnp.float32)).astype(jnp.bfloat16)
    return hi, lo


def nt(a, b):
    return lax.dot_general(a, b, NT_DIMS, preferred_element_type=jnp.float32)


def spread8(x):
    return jnp.broadcast_to(x, (8, TILE))


def total(terms):
    acc = terms[0]
    for term in terms[1:]:
        acc = acc + term
    return acc


def invert_tile(a_ref, i_ref, s_ref, out_ref, beside):
    row = lax.broadcasted_iota(jnp.int32, (TILE, TILE), 0)
    col = lax.broadcasted_iota(jnp.int32, (TILE, TILE), 1)
    i_ref[...] = (row == col).astype(jnp.float32)
    steps = TILE // 8
    for g in range(steps):
        base = 8 * g
        group = a_ref[base : base + 8, :]
        for k in range(8):
            s_ref[8 * k : 8 * k + 8, :] = spread8(group[:, base + k : base + k + 1])
        d = {}
        for k in range(8):
            for i in range(k, 8):
                d[i, k] = spread8(s_ref[8 * k + i : 8 * k + i + 1, :])
        ga = [spread8(a_ref[base + j : base + j + 1, :]) for j in range(8)]
        gi = [spread8(i_ref[base + j : base + j + 1, :]) for j in range(8)]
        rs = {}
        lo = {}
        for j in range(0, 8, 2):
            rs[j] = lax.rsqrt(d[j, j])
            det = lax.rsqrt(d[j, j] * d[j + 1, j + 1] - d[j + 1, j] * d[j + 1, j])
            rs[j + 1] = det * (d[j, j] * rs[j])
            lo[j + 1, j] = d[j + 1, j] * rs[j]
            for i in range(j + 2, 8):
                lo[i, j] = d[i, j] * rs[j]
                lo[i, j + 1] = (d[i, j + 1] - lo[i, j] * lo[j + 1, j]) * rs[j + 1]
            for k in range(j + 2, 8):
                for i in range(k, 8):
                    d[i, k] = d[i, k] - (lo[i, j] * lo[k, j] + lo[i, j + 1] * lo[k, j + 1])
        t = {}
        for j in range(8):
            t[j, j] = rs[j]
            for m in range(j):
                t[j, m] = -(total([lo[j, k] * t[k, m] for k in range(m, j)]) * rs[j])
        ui = [total([t[i, j] * gi[j] for j in range(i + 1)]) for i in range(8)]
        for i in range(8):
            out_ref[base + i : base + i + 1, :] = ui[i][0:1, :]
        if g < steps - 1:
            ua = [total([t[i, j] * ga[j] for j in range(i + 1)]) for i in range(8)]
            va = [total([t[i, j] * ua[i] for i in range(j, 8)]) for j in range(8)]
            vi = [total([t[i, j] * ui[i] for i in range(j, 8)]) for j in range(8)]
        for h in range(g + 1, steps):
            rows = slice(8 * h, 8 * h + 8)
            block = a_ref[rows, :]
            acc_a = block
            acc_i = i_ref[rows, :]
            for j in range(8):
                c = spread8(block[:, base + j : base + j + 1])
                acc_a = acc_a - c * va[j]
                acc_i = acc_i - c * vi[j]
            a_ref[rows, :] = acc_a
            i_ref[rows, :] = acc_i
        beside(g)


def unit_table(first, last):
    pairs = PANEL // 256
    table = np.full((pairs, SLOTS), (pairs - first) * 8, np.int32)
    for p in range(max(first, 1), last):
        units = [(q - first) * 8 + b for q in range(p + 1, pairs) for b in range(pairs) if b <= p - 1 or b >= q]
        table[p, : len(units)] = units
    return table.reshape(-1)


def factor_kernel(first, last, place_ref, unit_ref, *rest):
    tiles = PANEL // TILE
    pairs = tiles // 2
    if first == 0:
        source_ref, rest = rest[0], rest[1:]
    else:
        source_ref, oldh_ref, oldl_ref = rest[:3]
        rest = rest[3:]
    own_ref, xh_ref, xl_ref = rest[:3]
    rest = rest[3:]
    if last < pairs:
        next_ref, nexth_ref, nextl_ref = rest[:3]
        rest = rest[3:]
    m_ref, eh_ref, el_ref, a_ref, o_ref, i_ref, s_ref, t_ref, sem = rest
    if first == 0:
        for j in range(tiles):
            for i in range(tiles):
                spot = (j // 2, slice(i * TILE, (i + 1) * TILE), slice(j % 2 * TILE, (j % 2 + 1) * TILE))
                if i >= j:
                    m_ref[spot] = source_ref[i % 8 * 16 + j, i // 8].astype(jnp.float32)
                else:
                    m_ref[spot] = jnp.zeros((TILE, TILE), jnp.float32)
    else:
        loads = (
            pltpu.make_async_copy(source_ref, m_ref.at[pl.ds(0, pairs - first)], sem.at[0]),
            pltpu.make_async_copy(oldh_ref, eh_ref.at[(first - 1) % 2], sem.at[1]),
            pltpu.make_async_copy(oldl_ref, el_ref.at[(first - 1) % 2], sem.at[2]),
        )
        for load in loads:
            load.start()
        for load in loads:
            load.wait()
    own_ref[...] = jnp.zeros_like(own_ref)
    r = place_ref[0]
    c = place_ref[1]
    row = lax.broadcasted_iota(jnp.int32, (TILE, TILE), 0)
    col = lax.broadcasted_iota(jnp.int32, (TILE, TILE), 1)
    identity = (row == col).astype(jnp.float32)
    zero = jnp.zeros((TILE, TILE), jnp.bfloat16)

    def product(rows, cols, buf):
        lh, ll = eh_ref[buf, rows, :], el_ref[buf, rows, :]
        rh, rl = eh_ref[buf, cols, :], el_ref[buf, cols, :]
        return nt(lh, rh) + nt(lh, rl) + nt(ll, rh)

    def block_rows(b):
        return pl.ds(pl.multiple_of(b * 256, 256), 256)

    def tile_rows(i):
        return pl.ds(pl.multiple_of(i * TILE, TILE), TILE)

    def apply(code, buf):
        q = code // 8
        rows = block_rows(code % 8)
        cols = block_rows(jnp.minimum(q + first, pairs - 1))
        m_ref[q, rows, :] = m_ref[q, rows, :] - product(rows, cols, buf)

    def times(x, y):
        xh, xl = x
        yh, yl = y
        parts = nt(
            jnp.concatenate([xh, xl], 1),
            jnp.concatenate([jnp.concatenate([yh, yh], 1), jnp.concatenate([yl, yl], 1)], 0),
        )
        return parts[:, :TILE] + parts[:, TILE:]

    def keep_own(k, buf, half):
        @pl.when(k == c)
        def _():
            diag = times(split2(o_ref[...]), split2(t_ref[...]))
            diag = jnp.where(row >= col, diag, 0.0).astype(jnp.bfloat16)
            for a in range(2):
                i = r + a * 8
                src = eh_ref[buf, tile_rows(i), half * TILE : (half + 1) * TILE]
                own_ref[a] = jnp.where(i == k, diag, jnp.where(i > k, src, zero))

    def column(p, buf, half):
        inverse = split2(t_ref[...])
        lanes = slice(half * TILE, (half + 1) * TILE)
        for b in range(pairs):
            rows = slice(b * 256, (b + 1) * 256)
            eh, el = split2(times(split2(m_ref[p - first, rows, lanes]), inverse))
            eh_ref[buf, rows, lanes] = eh
            el_ref[buf, rows, lanes] = el

    def step(p, carry):
        local = p - first
        buf = p % 2
        old = 1 - buf
        k = 2 * p
        m_ref[local, tile_rows(k), TILE:] = jnp.zeros((TILE, TILE), jnp.float32)

        diag = m_ref[local, tile_rows(k), 0:TILE]
        diag = jnp.where(p > 0, diag - product(tile_rows(k), tile_rows(k), old), diag)
        a_ref[...] = diag
        o_ref[...] = diag

        def first_beside(g):
            if g < 8:
                rows = slice(g * 256, (g + 1) * 256)
                old_block = m_ref[local, rows, :]
                new_block = old_block - product(rows, block_rows(p), old)
                m_ref[local, rows, :] = jnp.where(p > 0, new_block, old_block)
            else:
                apply(unit_ref[p * SLOTS + g - 8], old)

        invert_tile(a_ref, i_ref, s_ref, t_ref, first_beside)
        m_ref[local, tile_rows(k), 0:TILE] = identity
        m_ref[local, tile_rows(k), TILE:] = jnp.zeros((TILE, TILE), jnp.float32)
        column(p, buf, 0)
        keep_own(k, buf, 0)

        def pair_product(rows):
            lanes = slice(0, TILE)
            return times(
                (eh_ref[buf, rows, lanes], el_ref[buf, rows, lanes]),
                (eh_ref[buf, tile_rows(k + 1), lanes], el_ref[buf, tile_rows(k + 1), lanes]),
            )

        diag = m_ref[local, tile_rows(k + 1), TILE:] - pair_product(tile_rows(k + 1))
        a_ref[...] = diag
        o_ref[...] = diag

        def second_beside(g):
            if g < 8:
                rows = slice(g * 256, (g + 1) * 256)
                m_ref[local, rows, TILE:] = m_ref[local, rows, TILE:] - pair_product(rows)
            apply(unit_ref[p * SLOTS + 8 + g], old)
            if g >= 12:
                apply(unit_ref[p * SLOTS + 12 + g], old)

        invert_tile(a_ref, i_ref, s_ref, t_ref, second_beside)
        m_ref[local, tile_rows(k + 1), TILE:] = identity
        column(p, buf, 1)
        keep_own(k + 1, buf, 1)
        eh_ref[buf, tile_rows(k + 1), 0:TILE] = zero
        el_ref[buf, tile_rows(k + 1), 0:TILE] = zero
        wide = pl.ds(pl.multiple_of(local * 256, 256), 256)
        depth = last * 256
        xh_ref[:, wide] = eh_ref[buf, 0:depth, :]
        xl_ref[:, wide] = el_ref[buf, 0:depth, :]
        return carry

    lax.fori_loop(first, last, step, 0)
    if last < pairs:
        next_ref[...] = m_ref[last - first : pairs - first]
        nexth_ref[...] = eh_ref[(last - 1) % 2]
        nextl_ref[...] = el_ref[(last - 1) % 2]


def factor_stage(first, last, place, *sources):
    pairs = PANEL // 256
    vm = pl.BlockSpec(memory_space=pltpu.VMEM)
    smem = pl.BlockSpec(memory_space=pltpu.SMEM)
    wide = (last - first) * 256
    out_shape = [
        jax.ShapeDtypeStruct((2, TILE, TILE), jnp.bfloat16),
        jax.ShapeDtypeStruct((last * 256, wide), jnp.bfloat16),
        jax.ShapeDtypeStruct((last * 256, wide), jnp.bfloat16),
    ]
    if last < pairs:
        out_shape.append(jax.ShapeDtypeStruct((pairs - last, PANEL, 256), jnp.float32))
        out_shape += [jax.ShapeDtypeStruct((PANEL, 256), jnp.bfloat16)] * 2
    tile = pltpu.VMEM((TILE, TILE), jnp.float32)
    return pl.pallas_call(
        functools.partial(factor_kernel, first, last),
        out_shape=tuple(out_shape),
        in_specs=[smem, smem] + ([vm] if first == 0 else [pl.BlockSpec(memory_space=pl.ANY)] * 3),
        out_specs=tuple(vm for _ in out_shape),
        scratch_shapes=[
            pltpu.VMEM((pairs - first + 1, PANEL, 256), jnp.float32),
            pltpu.VMEM((2, PANEL, 256), jnp.bfloat16),
            pltpu.VMEM((2, PANEL, 256), jnp.bfloat16),
            tile,
            tile,
            tile,
            tile,
            tile,
            pltpu.SemaphoreType.DMA((3,)),
        ],
        compiler_params=pltpu.CompilerParams(vmem_limit_bytes=60 * 1024 * 1024),
        cost_estimate=pl.CostEstimate(flops=60_000_000_000, bytes_accessed=24_000_000, transcendentals=0),
        name="factor_corner",
    )(place, jnp.asarray(unit_table(first, last)), *sources)


def pack_kernel(slot_ref, child_ref, head_ref, packed_ref):
    packed_ref[:, CAP * TILE :, :] = head_ref[...]

    def move(t, carry):
        slot = slot_ref[t]
        rows = pl.ds(pl.multiple_of(slot % CAP * TILE, TILE), TILE)
        packed_ref[slot // CAP, rows, :] = child_ref[t]
        return carry

    lax.fori_loop(0, child_ref.shape[0], move, 0)


def pack(slots, child_tiles, head):
    vm = pl.BlockSpec(memory_space=pltpu.VMEM)
    return pl.pallas_call(
        pack_kernel,
        out_shape=jax.ShapeDtypeStruct((head.shape[0], CAP * TILE + HEAD, TILE), jnp.bfloat16),
        in_specs=[pl.BlockSpec(memory_space=pltpu.SMEM), vm, vm],
        out_specs=vm,
        compiler_params=pltpu.CompilerParams(vmem_limit_bytes=32 * 1024 * 1024),
        cost_estimate=pl.CostEstimate(flops=0, bytes_accessed=16_000_000, transcendentals=0),
        name="pack_tiles",
    )(slots, child_tiles, head)


def extend_kernel(id_ref, front_ref, arrived_ref, out_ref, panel_ref, acc_ref):
    cols_local = front_ref.shape[1] // TILE
    rows_local = front_ref.shape[0]
    acc_ref[0:rows_local, :] = front_ref[...].astype(jnp.float32)

    def add(s, carry):
        local = id_ref[s]
        used = local >= 0
        top = jnp.where(used, local // cols_local * TILE, rows_local)
        left = jnp.where(used, local % cols_local * TILE, 0)
        spot = (pl.ds(pl.multiple_of(top, TILE), TILE), pl.ds(pl.multiple_of(left, TILE), TILE))
        rows = pl.ds(pl.multiple_of(s % CAP * TILE, TILE), TILE)
        acc_ref[spot] = acc_ref[spot] + arrived_ref[s // CAP, rows, :].astype(jnp.float32)
        return carry

    lax.fori_loop(0, CAP * arrived_ref.shape[0], add, 0, unroll=4)
    summed = acc_ref[0:rows_local, :].astype(jnp.bfloat16)
    out_ref[...] = summed
    panel_ref[...] = summed[2 * TILE :, 0:TILE]


def extend(ids, front, arrived):
    vm = pl.BlockSpec(memory_space=pltpu.VMEM)
    return pl.pallas_call(
        extend_kernel,
        out_shape=(
            jax.ShapeDtypeStruct(front.shape, jnp.bfloat16),
            jax.ShapeDtypeStruct((front.shape[0] - 2 * TILE, TILE), jnp.bfloat16),
        ),
        in_specs=[pl.BlockSpec(memory_space=pltpu.SMEM), vm, vm],
        out_specs=(vm, vm),
        scratch_shapes=[pltpu.VMEM((front.shape[0] + TILE, front.shape[1]), jnp.float32)],
        compiler_params=pltpu.CompilerParams(vmem_limit_bytes=48 * 1024 * 1024),
        cost_estimate=pl.CostEstimate(flops=10_000_000, bytes_accessed=30_000_000, transcendentals=0),
        name="extend_add",
    )(ids, front, arrived)


def finish_kernel(
    place_ref, xh1_ref, xl1_ref, xh2_ref, xl2_ref, row_ref, col_ref, own1_ref, own2_ref, assembled_ref, out_ref, a_ref, p_ref, sum_ref, acc_ref
):
    step = pl.program_id(0)
    steps = PANEL // (2 * TILE)
    rows_low = row_ref.shape[1] * TILE
    cols_low = col_ref.shape[1] * TILE
    total = rows_low + cols_low
    cols_local = assembled_ref.shape[1] // TILE
    c = place_ref[1]
    width = 2 * TILE

    @pl.when(step == 0)
    def _():
        top = 2 * TILE * cols_local
        out_ref[0:top, :] = jnp.zeros((top, TILE), jnp.float32)
        for a in range(2):
            rows = pl.ds(a * TILE * cols_local, TILE, stride=cols_local)
            out_ref[rows, :] = own1_ref[a].astype(jnp.float32) + own2_ref[a].astype(jnp.float32)
        acc_ref[...] = assembled_ref[2 * TILE :, TILE:].astype(jnp.float32)

    for piece in range(2):
        lanes = slice(piece * TILE, (piece + 1) * TILE)
        a_ref[step, 0:rows_low, lanes] = row_ref[piece].reshape(rows_low, TILE)
        a_ref[step, rows_low:total, lanes] = col_ref[piece].reshape(cols_low, TILE)

    def solve_with(xh_ref, xl_ref):
        def part(first, count):
            rows = pl.ds(pl.multiple_of(first * width, width), count * width)
            a = jnp.concatenate([a_ref[first + n] for n in range(count)], 1)
            return jnp.dot(a, xh_ref[rows, :], preferred_element_type=jnp.float32) + jnp.dot(
                a, xl_ref[rows, :], preferred_element_type=jnp.float32
            )

        odd = (step + 1) % 2

        @pl.when(odd == 1)
        def _():
            sum_ref[...] = part(0, 1)

        @pl.when(odd == 0)
        def _():
            sum_ref[...] = jnp.zeros_like(sum_ref)

        def solve(n, carry):
            sum_ref[...] = sum_ref[...] + part(odd + 2 * n, 2)
            return carry

        lax.fori_loop(0, (step + 1) // 2, solve, 0)
        p_ref[:, pl.ds(pl.multiple_of(step % 2 * width, width), width)] = sum_ref[...].astype(jnp.bfloat16)

    mid = xh1_ref.shape[0] // width

    @pl.when(step < mid)
    def _():
        solve_with(xh1_ref, xl1_ref)

    @pl.when(step >= mid)
    def _():
        solve_with(xh2_ref, xl2_ref)

    @pl.when(step == c // 2)
    def _():
        lane = pl.multiple_of(c % 4 * TILE, TILE)
        rows = pl.ds(2 * TILE * cols_local, rows_low, stride=cols_local)
        out_ref[rows, :] = p_ref[0:rows_low, pl.ds(lane, TILE)].astype(jnp.float32)

    def update(b, carry):
        rows = pl.ds(pl.multiple_of(b * chunk, chunk), chunk)
        acc_ref[rows, :] = acc_ref[rows, :] - nt(p_ref[rows, :], p_ref[rows_low:total, :])
        return carry

    chunk = rows_low

    @pl.when(step % 2 == 1)
    def _():
        lax.fori_loop(0, 1, update, 0)

    @pl.when(step == steps - 1)
    def _():
        def write(t, carry):
            lanes = pl.ds(pl.multiple_of((t - 1) * TILE, TILE), TILE)
            out_ref[pl.ds(2 * TILE * cols_local + t, rows_low, stride=cols_local), :] = acc_ref[:, lanes]
            return carry

        lax.fori_loop(1, cols_local, write, 0)


def finish(place, x1, x2, row_raw, col_raw, own1, own2, assembled):
    width = 2 * TILE
    steps = PANEL // width
    mid = x1[0].shape[1] // width
    tiles_row = row_raw.shape[1]
    tiles_col = col_raw.shape[1]
    total = (tiles_row + tiles_col) * TILE
    vm = pl.BlockSpec(memory_space=pltpu.VMEM)
    early = pl.BlockSpec((mid * width, width), lambda s: (0, jnp.minimum(s, mid - 1)))
    late = pl.BlockSpec((PANEL, width), lambda s: (0, jnp.maximum(s - mid, 0)))
    return pl.pallas_call(
        finish_kernel,
        grid=(steps,),
        out_shape=jax.ShapeDtypeStruct((assembled.shape[0] * assembled.shape[1] // TILE, TILE), jnp.float32),
        in_specs=[
            pl.BlockSpec(memory_space=pltpu.SMEM),
            early,
            early,
            late,
            late,
            pl.BlockSpec((2, tiles_row, TILE, TILE), lambda s: (s, 0, 0, 0)),
            pl.BlockSpec((2, tiles_col, TILE, TILE), lambda s: (s, 0, 0, 0)),
            vm,
            vm,
            vm,
        ],
        out_specs=vm,
        scratch_shapes=[
            pltpu.VMEM((steps, total, width), jnp.bfloat16),
            pltpu.VMEM((total, 2 * width), jnp.bfloat16),
            pltpu.VMEM((total, width), jnp.float32),
            pltpu.VMEM((tiles_row * TILE, tiles_col * TILE), jnp.float32),
        ],
        compiler_params=pltpu.CompilerParams(
            vmem_limit_bytes=56 * 1024 * 1024, dimension_semantics=("arbitrary",)
        ),
        cost_estimate=pl.CostEstimate(flops=40_000_000_000, bytes_accessed=50_000_000, transcendentals=0),
        name="solve_update",
    )(place, *x1, *x2, row_raw, col_raw, own1, own2, assembled)


def per_device(front, child_tiles, tile_map):
    rows_local = front.shape[0]
    cols_local = front.shape[3]
    row_count = lax.axis_size("row")
    col_count = lax.axis_size("col")
    device_count = row_count * col_count
    row_index = lax.axis_index("row")
    col_index = lax.axis_index("col")
    both = ("row", "col")
    corner = front[0:2, 0, :, 0, 0, :]
    corner = lax.all_gather(corner, both, axis=0, tiled=False)

    owners = tile_map[:, 0] % row_count * col_count + tile_map[:, 1] % col_count
    local_ids = tile_map[:, 0] // row_count * cols_local + tile_map[:, 1] // col_count
    owner_hits = (owners[:, None] == jnp.arange(device_count)[None, :]).astype(jnp.int32)
    slot_rank = jnp.sum(jnp.cumsum(owner_hits, 0) * owner_hits, 1) - 1
    slot_index = owners * CAP + slot_rank
    targets = jnp.full((device_count * CAP,), -1, jnp.int32).at[slot_index].set(local_ids)
    head = jnp.pad(
        targets.astype(jnp.bfloat16).reshape(device_count, 1, CAP), ((0, 0), (0, HEAD - 1), (0, TILE - CAP))
    )
    arrived = lax.all_to_all(
        pack(slot_index, child_tiles, head), both, split_axis=0, concat_axis=0, tiled=True
    )
    arrived_ids = arrived[:, CAP * TILE, 0:CAP].astype(jnp.int32).reshape(device_count * CAP)
    assembled, panel = extend(arrived_ids, front.reshape(rows_local * TILE, cols_local * TILE), arrived)
    corner, panel = lax.optimization_barrier((corner, panel))

    place = jnp.stack([row_index, col_index]).astype(jnp.int32)
    own1, xh1, xl1, *state = factor_stage(0, SPLIT, place, corner)
    low_tiles = rows_local - 2
    panel = panel.reshape(low_tiles, TILE, TILE)
    row_raw = lax.all_gather(panel, "col", axis=0, tiled=False)
    split_panel = panel.reshape(low_tiles // 2, 2, TILE, TILE)
    halves = (split_panel[:, 0], split_panel[:, 1])
    parity = col_index % 2
    received = []
    for k in range(2):
        pairs = []
        for r in range(row_count):
            for c in range(col_count):
                h = (c % 2) ^ k
                pairs.append((r * col_count + c, (c // 2) * col_count + row_count * h + r))
        outgoing = jnp.where(parity == k, halves[0], halves[1])
        received.append(lax.ppermute(outgoing, both, pairs))
    high = col_index // row_count
    first = jnp.where(high == 0, received[0], received[1])
    second = jnp.where(high == 0, received[1], received[0])
    pieces = jnp.broadcast_to(jnp.stack([first, second]), (row_count, 2) + first.shape)
    *state, pieces = lax.optimization_barrier((*state, pieces))
    col_raw = lax.all_to_all(
        pieces, "row", split_axis=0, concat_axis=0, tiled=True
    ).reshape(col_count, low_tiles // 2, TILE, TILE)
    own2, xh2, xl2 = factor_stage(SPLIT, PANEL // 256, place, *state)
    out = finish(place, (xh1, xl1), (xh2, xl2), row_raw, col_raw, own1, own2, assembled)
    return out.reshape(rows_local, 1, TILE, cols_local, 1, TILE)


def solution(mesh):
    in_specs = (
        P(None, "row", None, None, "col", None),
        P(("row", "col"), None, None),
        P(("row", "col"), None),
    )
    out_specs = P(None, "row", None, None, "col", None)
    return jax.shard_map(
        per_device, mesh=mesh, in_specs=in_specs, out_specs=out_specs, check_vma=False
    )
```

```python
import functools
import numpy as np
import jax
import jax.numpy as jnp
from jax import lax
from jax.experimental import pallas as pl
from jax.experimental.pallas import tpu as pltpu
from jax.sharding import PartitionSpec as P

CAP = 2
HEAD = 16
PANEL = 2048
TILE = 128
NT_DIMS = (((1,), (1,)), ((), ()))
SLOTS = 32


def split2(x):
    hi = x.astype(jnp.bfloat16)
    lo = (x - hi.astype(jnp.float32)).astype(jnp.bfloat16)
    return hi, lo


def nt(a, b):
    return lax.dot_general(a, b, NT_DIMS, preferred_element_type=jnp.float32)


def spread8(x):
    return jnp.broadcast_to(x, (8, TILE))


def total(terms):
    acc = terms[0]
    for term in terms[1:]:
        acc = acc + term
    return acc


def invert_tile(a_ref, i_ref, s_ref, out_ref, beside):
    row = lax.broadcasted_iota(jnp.int32, (TILE, TILE), 0)
    col = lax.broadcasted_iota(jnp.int32, (TILE, TILE), 1)
    i_ref[...] = (row == col).astype(jnp.float32)
    steps = TILE // 8
    for g in range(steps):
        base = 8 * g
        group = a_ref[base : base + 8, :]
        for k in range(8):
            s_ref[8 * k : 8 * k + 8, :] = spread8(group[:, base + k : base + k + 1])
        d = {}
        for k in range(8):
            for i in range(k, 8):
                d[i, k] = spread8(s_ref[8 * k + i : 8 * k + i + 1, :])
        ga = [spread8(a_ref[base + j : base + j + 1, :]) for j in range(8)]
        gi = [spread8(i_ref[base + j : base + j + 1, :]) for j in range(8)]
        rs = {}
        lo = {}
        for j in range(0, 8, 2):
            rs[j] = lax.rsqrt(d[j, j])
            det = lax.rsqrt(d[j, j] * d[j + 1, j + 1] - d[j + 1, j] * d[j + 1, j])
            rs[j + 1] = det * (d[j, j] * rs[j])
            lo[j + 1, j] = d[j + 1, j] * rs[j]
            for i in range(j + 2, 8):
                lo[i, j] = d[i, j] * rs[j]
                lo[i, j + 1] = (d[i, j + 1] - lo[i, j] * lo[j + 1, j]) * rs[j + 1]
            for k in range(j + 2, 8):
                for i in range(k, 8):
                    d[i, k] = d[i, k] - (lo[i, j] * lo[k, j] + lo[i, j + 1] * lo[k, j + 1])
        t = {}
        for j in range(8):
            t[j, j] = rs[j]
            for m in range(j):
                t[j, m] = -(total([lo[j, k] * t[k, m] for k in range(m, j)]) * rs[j])
        ui = [total([t[i, j] * gi[j] for j in range(i + 1)]) for i in range(8)]
        for i in range(8):
            out_ref[base + i : base + i + 1, :] = ui[i][0:1, :]
        if g < steps - 1:
            ua = [total([t[i, j] * ga[j] for j in range(i + 1)]) for i in range(8)]
            va = [total([t[i, j] * ua[i] for i in range(j, 8)]) for j in range(8)]
            vi = [total([t[i, j] * ui[i] for i in range(j, 8)]) for j in range(8)]
        for h in range(g + 1, steps):
            rows = slice(8 * h, 8 * h + 8)
            block = a_ref[rows, :]
            acc_a = block
            acc_i = i_ref[rows, :]
            for j in range(8):
                c = spread8(block[:, base + j : base + j + 1])
                acc_a = acc_a - c * va[j]
                acc_i = acc_i - c * vi[j]
            a_ref[rows, :] = acc_a
            i_ref[rows, :] = acc_i
        beside(g)


def unit_table(first, last):
    pairs = PANEL // 256
    table = np.full((pairs, SLOTS), (pairs - first) * 8, np.int32)
    for p in range(max(first, 1), last):
        units = [(q - first) * 8 + b for q in range(p + 1, pairs) for b in range(pairs) if b <= p - 1 or b >= q]
        table[p, : len(units)] = units
    return table.reshape(-1)


def factor_kernel(first, last, place_ref, unit_ref, *rest):
    tiles = PANEL // TILE
    pairs = tiles // 2
    source_ref, own_ref, xh_ref, xl_ref, *rest = rest
    m_ref, eh_ref, el_ref, a_ref, o_ref, i_ref, s_ref, t_ref, sem = rest
    for j in range(tiles):
        for i in range(tiles):
            spot = (j // 2, slice(i * TILE, (i + 1) * TILE), slice(j % 2 * TILE, (j % 2 + 1) * TILE))
            if i >= j:
                m_ref[spot] = source_ref[i % 8 * 16 + j, i // 8].astype(jnp.float32)
            else:
                m_ref[spot] = jnp.zeros((TILE, TILE), jnp.float32)
    own_ref[...] = jnp.zeros_like(own_ref)
    r = place_ref[0]
    c = place_ref[1]
    row = lax.broadcasted_iota(jnp.int32, (TILE, TILE), 0)
    col = lax.broadcasted_iota(jnp.int32, (TILE, TILE), 1)
    identity = (row == col).astype(jnp.float32)
    zero = jnp.zeros((TILE, TILE), jnp.bfloat16)

    def product(rows, cols, buf):
        lh, ll = eh_ref[buf, rows, :], el_ref[buf, rows, :]
        rh, rl = eh_ref[buf, cols, :], el_ref[buf, cols, :]
        return nt(lh, rh) + nt(lh, rl) + nt(ll, rh)

    def block_rows(b):
        return pl.ds(pl.multiple_of(b * 256, 256), 256)

    def tile_rows(i):
        return pl.ds(pl.multiple_of(i * TILE, TILE), TILE)

    def apply(code, buf):
        q = code // 8
        rows = block_rows(code % 8)
        cols = block_rows(jnp.minimum(q + first, pairs - 1))
        m_ref[q, rows, :] = m_ref[q, rows, :] - product(rows, cols, buf)

    def times(x, y):
        xh, xl = x
        yh, yl = y
        parts = nt(
            jnp.concatenate([xh, xl], 1),
            jnp.concatenate([jnp.concatenate([yh, yh], 1), jnp.concatenate([yl, yl], 1)], 0),
        )
        return parts[:, :TILE] + parts[:, TILE:]

    def keep_own(k, buf, half):
        @pl.when(k == c)
        def _():
            diag = times(split2(o_ref[...]), split2(t_ref[...]))
            diag = jnp.where(row >= col, diag, 0.0).astype(jnp.bfloat16)
            for a in range(2):
                i = r + a * 8
                src = eh_ref[buf, tile_rows(i), half * TILE : (half + 1) * TILE]
                own_ref[a] = jnp.where(i == k, diag, jnp.where(i > k, src, zero))

    def column(p, buf, half):
        inverse = split2(t_ref[...])
        lanes = slice(half * TILE, (half + 1) * TILE)
        for b in range(pairs):
            rows = slice(b * 256, (b + 1) * 256)
            eh, el = split2(times(split2(m_ref[p - first, rows, lanes]), inverse))
            eh_ref[buf, rows, lanes] = eh
            el_ref[buf, rows, lanes] = el

    def keep_inverse(p, buf):
        wide = pl.ds(pl.multiple_of(p * 256, 256), 256)
        return (
            pltpu.make_async_copy(eh_ref.at[buf], xh_ref.at[:, wide], sem.at[0, buf]),
            pltpu.make_async_copy(el_ref.at[buf], xl_ref.at[:, wide], sem.at[1, buf]),
        )

    def step(p, carry):
        local = p - first
        buf = p % 2
        old = 1 - buf
        k = 2 * p
        m_ref[local, tile_rows(k), TILE:] = jnp.zeros((TILE, TILE), jnp.float32)

        diag = m_ref[local, tile_rows(k), 0:TILE]
        diag = jnp.where(p > 0, diag - product(tile_rows(k), tile_rows(k), old), diag)
        a_ref[...] = diag
        o_ref[...] = diag

        def first_beside(g):
            if g < 8:
                rows = slice(g * 256, (g + 1) * 256)
                old_block = m_ref[local, rows, :]
                new_block = old_block - product(rows, block_rows(p), old)
                m_ref[local, rows, :] = jnp.where(p > 0, new_block, old_block)
            else:
                apply(unit_ref[p * SLOTS + g - 8], old)

        invert_tile(a_ref, i_ref, s_ref, t_ref, first_beside)
        m_ref[local, tile_rows(k), 0:TILE] = identity
        m_ref[local, tile_rows(k), TILE:] = jnp.zeros((TILE, TILE), jnp.float32)
        @pl.when(p >= 2)
        def _():
            for copy in keep_inverse(p - 2, buf):
                copy.wait()

        column(p, buf, 0)
        keep_own(k, buf, 0)

        def pair_product(rows):
            lanes = slice(0, TILE)
            return times(
                (eh_ref[buf, rows, lanes], el_ref[buf, rows, lanes]),
                (eh_ref[buf, tile_rows(k + 1), lanes], el_ref[buf, tile_rows(k + 1), lanes]),
            )

        diag = m_ref[local, tile_rows(k + 1), TILE:] - pair_product(tile_rows(k + 1))
        a_ref[...] = diag
        o_ref[...] = diag

        def second_beside(g):
            if g < 8:
                rows = slice(g * 256, (g + 1) * 256)
                m_ref[local, rows, TILE:] = m_ref[local, rows, TILE:] - pair_product(rows)
            apply(unit_ref[p * SLOTS + 8 + g], old)
            if g >= 12:
                apply(unit_ref[p * SLOTS + 12 + g], old)

        invert_tile(a_ref, i_ref, s_ref, t_ref, second_beside)
        m_ref[local, tile_rows(k + 1), TILE:] = identity
        column(p, buf, 1)
        keep_own(k + 1, buf, 1)
        eh_ref[buf, tile_rows(k + 1), 0:TILE] = zero
        el_ref[buf, tile_rows(k + 1), 0:TILE] = zero
        for copy in keep_inverse(p, buf):
            copy.start()
        return carry

    lax.fori_loop(first, last, step, 0)
    for p in (pairs - 2, pairs - 1):
        for copy in keep_inverse(p, p % 2):
            copy.wait()


def factor_corner(place, corner):
    pairs = PANEL // 256
    vm = pl.BlockSpec(memory_space=pltpu.VMEM)
    hbm = pl.BlockSpec(memory_space=pl.ANY)
    smem = pl.BlockSpec(memory_space=pltpu.SMEM)
    tile = pltpu.VMEM((TILE, TILE), jnp.float32)
    return pl.pallas_call(
        functools.partial(factor_kernel, 0, pairs),
        out_shape=(
            jax.ShapeDtypeStruct((2, TILE, TILE), jnp.bfloat16),
            jax.ShapeDtypeStruct((PANEL, PANEL), jnp.bfloat16),
            jax.ShapeDtypeStruct((PANEL, PANEL), jnp.bfloat16),
        ),
        in_specs=[smem, smem, vm],
        out_specs=(vm, hbm, hbm),
        scratch_shapes=[
            pltpu.VMEM((pairs + 1, PANEL, 256), jnp.float32),
            pltpu.VMEM((2, PANEL, 256), jnp.bfloat16),
            pltpu.VMEM((2, PANEL, 256), jnp.bfloat16),
            tile,
            tile,
            tile,
            tile,
            tile,
            pltpu.SemaphoreType.DMA((2, 2)),
        ],
        compiler_params=pltpu.CompilerParams(vmem_limit_bytes=56 * 1024 * 1024),
        cost_estimate=pl.CostEstimate(flops=90_000_000_000, bytes_accessed=24_000_000, transcendentals=0),
        name="factor_corner",
    )(place, jnp.asarray(unit_table(0, pairs)), corner)


def pack_kernel(slot_ref, child_ref, head_ref, packed_ref):
    packed_ref[:, CAP * TILE :, :] = head_ref[...]

    def move(t, carry):
        slot = slot_ref[t]
        rows = pl.ds(pl.multiple_of(slot % CAP * TILE, TILE), TILE)
        packed_ref[slot // CAP, rows, :] = child_ref[t]
        return carry

    lax.fori_loop(0, child_ref.shape[0], move, 0)


def pack(slots, child_tiles, head):
    vm = pl.BlockSpec(memory_space=pltpu.VMEM)
    return pl.pallas_call(
        pack_kernel,
        out_shape=jax.ShapeDtypeStruct((head.shape[0], CAP * TILE + HEAD, TILE), jnp.bfloat16),
        in_specs=[pl.BlockSpec(memory_space=pltpu.SMEM), vm, vm],
        out_specs=vm,
        compiler_params=pltpu.CompilerParams(vmem_limit_bytes=32 * 1024 * 1024),
        cost_estimate=pl.CostEstimate(flops=0, bytes_accessed=16_000_000, transcendentals=0),
        name="pack_tiles",
    )(slots, child_tiles, head)


def extend_kernel(id_ref, front_ref, arrived_ref, out_ref, panel_ref, acc_ref):
    cols_local = front_ref.shape[1] // TILE
    rows_local = front_ref.shape[0]
    acc_ref[0:rows_local, :] = front_ref[...].astype(jnp.float32)

    def add(s, carry):
        local = id_ref[s]
        used = local >= 0
        top = jnp.where(used, local // cols_local * TILE, rows_local)
        left = jnp.where(used, local % cols_local * TILE, 0)
        spot = (pl.ds(pl.multiple_of(top, TILE), TILE), pl.ds(pl.multiple_of(left, TILE), TILE))
        rows = pl.ds(pl.multiple_of(s % CAP * TILE, TILE), TILE)
        acc_ref[spot] = acc_ref[spot] + arrived_ref[s // CAP, rows, :].astype(jnp.float32)
        return carry

    lax.fori_loop(0, CAP * arrived_ref.shape[0], add, 0, unroll=4)
    summed = acc_ref[0:rows_local, :].astype(jnp.bfloat16)
    out_ref[...] = summed
    panel_ref[...] = summed[2 * TILE :, 0:TILE]


def extend(ids, front, arrived):
    vm = pl.BlockSpec(memory_space=pltpu.VMEM)
    return pl.pallas_call(
        extend_kernel,
        out_shape=(
            jax.ShapeDtypeStruct(front.shape, jnp.bfloat16),
            jax.ShapeDtypeStruct((front.shape[0] - 2 * TILE, TILE), jnp.bfloat16),
        ),
        in_specs=[pl.BlockSpec(memory_space=pltpu.SMEM), vm, vm],
        out_specs=(vm, vm),
        scratch_shapes=[pltpu.VMEM((front.shape[0] + TILE, front.shape[1]), jnp.float32)],
        compiler_params=pltpu.CompilerParams(vmem_limit_bytes=48 * 1024 * 1024),
        cost_estimate=pl.CostEstimate(flops=10_000_000, bytes_accessed=30_000_000, transcendentals=0),
        name="extend_add",
    )(ids, front, arrived)


def finish_kernel(
    place_ref, xh_ref, xl_ref, row_ref, col_ref, own_ref, assembled_ref, out_ref, a_ref, p_ref, sum_ref, acc_ref
):
    step = pl.program_id(0)
    steps = PANEL // (2 * TILE)
    rows_low = row_ref.shape[1] * TILE
    cols_low = col_ref.shape[1] * TILE
    total = rows_low + cols_low
    cols_local = assembled_ref.shape[1] // TILE
    c = place_ref[1]
    width = 2 * TILE

    @pl.when(step == 0)
    def _():
        top = 2 * TILE * cols_local
        out_ref[0:top, :] = jnp.zeros((top, TILE), jnp.float32)
        for a in range(2):
            rows = pl.ds(a * TILE * cols_local, TILE, stride=cols_local)
            out_ref[rows, :] = own_ref[a].astype(jnp.float32)
        acc_ref[...] = assembled_ref[2 * TILE :, TILE:].astype(jnp.float32)

    for piece in range(2):
        lanes = slice(piece * TILE, (piece + 1) * TILE)
        a_ref[step, 0:rows_low, lanes] = row_ref[piece].reshape(rows_low, TILE)
        a_ref[step, rows_low:total, lanes] = col_ref[piece].reshape(cols_low, TILE)

    def part(first, count):
        rows = pl.ds(pl.multiple_of(first * width, width), count * width)
        a = jnp.concatenate([a_ref[first + n] for n in range(count)], 1)
        return jnp.dot(a, xh_ref[rows, :], preferred_element_type=jnp.float32) + jnp.dot(
            a, xl_ref[rows, :], preferred_element_type=jnp.float32
        )

    odd = (step + 1) % 2

    @pl.when(odd == 1)
    def _():
        sum_ref[...] = part(0, 1)

    @pl.when(odd == 0)
    def _():
        sum_ref[...] = jnp.zeros_like(sum_ref)

    def solve(n, carry):
        sum_ref[...] = sum_ref[...] + part(odd + 2 * n, 2)
        return carry

    lax.fori_loop(0, (step + 1) // 2, solve, 0)
    p_ref[:, pl.ds(pl.multiple_of(step % 2 * width, width), width)] = sum_ref[...].astype(jnp.bfloat16)

    @pl.when(step == c // 2)
    def _():
        lane = pl.multiple_of(c % 4 * TILE, TILE)
        rows = pl.ds(2 * TILE * cols_local, rows_low, stride=cols_local)
        out_ref[rows, :] = p_ref[0:rows_low, pl.ds(lane, TILE)].astype(jnp.float32)

    def update(b, carry):
        rows = pl.ds(pl.multiple_of(b * chunk, chunk), chunk)
        acc_ref[rows, :] = acc_ref[rows, :] - nt(p_ref[rows, :], p_ref[rows_low:total, :])
        return carry

    chunk = rows_low

    @pl.when(step % 2 == 1)
    def _():
        lax.fori_loop(0, 1, update, 0)

    @pl.when(step == steps - 1)
    def _():
        def write(t, carry):
            lanes = pl.ds(pl.multiple_of((t - 1) * TILE, TILE), TILE)
            out_ref[pl.ds(2 * TILE * cols_local + t, rows_low, stride=cols_local), :] = acc_ref[:, lanes]
            return carry

        lax.fori_loop(1, cols_local, write, 0)


def finish(place, xh, xl, row_raw, col_raw, own, assembled):
    width = 2 * TILE
    steps = PANEL // width
    tiles_row = row_raw.shape[1]
    tiles_col = col_raw.shape[1]
    total = (tiles_row + tiles_col) * TILE
    vm = pl.BlockSpec(memory_space=pltpu.VMEM)
    inverse = pl.BlockSpec((PANEL, width), lambda s: (0, s))
    return pl.pallas_call(
        finish_kernel,
        grid=(steps,),
        out_shape=jax.ShapeDtypeStruct((assembled.shape[0] * assembled.shape[1] // TILE, TILE), jnp.float32),
        in_specs=[
            pl.BlockSpec(memory_space=pltpu.SMEM),
            inverse,
            inverse,
            pl.BlockSpec((2, tiles_row, TILE, TILE), lambda s: (s, 0, 0, 0)),
            pl.BlockSpec((2, tiles_col, TILE, TILE), lambda s: (s, 0, 0, 0)),
            vm,
            vm,
        ],
        out_specs=vm,
        scratch_shapes=[
            pltpu.VMEM((steps, total, width), jnp.bfloat16),
            pltpu.VMEM((total, 2 * width), jnp.bfloat16),
            pltpu.VMEM((total, width), jnp.float32),
            pltpu.VMEM((tiles_row * TILE, tiles_col * TILE), jnp.float32),
        ],
        compiler_params=pltpu.CompilerParams(
            vmem_limit_bytes=56 * 1024 * 1024, dimension_semantics=("arbitrary",)
        ),
        cost_estimate=pl.CostEstimate(flops=40_000_000_000, bytes_accessed=50_000_000, transcendentals=0),
        name="solve_update",
    )(place, xh, xl, row_raw, col_raw, own, assembled)


def per_device(front, child_tiles, tile_map):
    rows_local = front.shape[0]
    cols_local = front.shape[3]
    row_count = lax.axis_size("row")
    col_count = lax.axis_size("col")
    device_count = row_count * col_count
    row_index = lax.axis_index("row")
    col_index = lax.axis_index("col")
    both = ("row", "col")
    corner = front[0:2, 0, :, 0, 0, :]
    corner = lax.all_gather(corner, both, axis=0, tiled=False)

    owners = tile_map[:, 0] % row_count * col_count + tile_map[:, 1] % col_count
    local_ids = tile_map[:, 0] // row_count * cols_local + tile_map[:, 1] // col_count
    owner_hits = (owners[:, None] == jnp.arange(device_count)[None, :]).astype(jnp.int32)
    slot_rank = jnp.sum(jnp.cumsum(owner_hits, 0) * owner_hits, 1) - 1
    slot_index = owners * CAP + slot_rank
    targets = jnp.full((device_count * CAP,), -1, jnp.int32).at[slot_index].set(local_ids)
    head = jnp.pad(
        targets.astype(jnp.bfloat16).reshape(device_count, 1, CAP), ((0, 0), (0, HEAD - 1), (0, TILE - CAP))
    )
    arrived = lax.all_to_all(
        pack(slot_index, child_tiles, head), both, split_axis=0, concat_axis=0, tiled=True
    )
    arrived_ids = arrived[:, CAP * TILE, 0:CAP].astype(jnp.int32).reshape(device_count * CAP)
    assembled, panel = extend(arrived_ids, front.reshape(rows_local * TILE, cols_local * TILE), arrived)
    low_tiles = rows_local - 2
    panel = panel.reshape(low_tiles, TILE, TILE)
    row_raw = lax.all_gather(panel, "col", axis=0, tiled=False)
    split_panel = panel.reshape(low_tiles // 2, 2, TILE, TILE)
    halves = (split_panel[:, 0], split_panel[:, 1])
    parity = col_index % 2
    received = []
    for k in range(2):
        pairs = []
        for r in range(row_count):
            for c in range(col_count):
                h = (c % 2) ^ k
                pairs.append((r * col_count + c, (c // 2) * col_count + row_count * h + r))
        outgoing = jnp.where(parity == k, halves[0], halves[1])
        received.append(lax.ppermute(outgoing, both, pairs))
    high = col_index // row_count
    first = jnp.where(high == 0, received[0], received[1])
    second = jnp.where(high == 0, received[1], received[0])
    pieces = jnp.broadcast_to(jnp.stack([first, second]), (row_count, 2) + first.shape)
    corner, pieces = lax.optimization_barrier((corner, pieces))
    col_raw = lax.all_to_all(
        pieces, "row", split_axis=0, concat_axis=0, tiled=True
    ).reshape(col_count, low_tiles // 2, TILE, TILE)
    place = jnp.stack([row_index, col_index]).astype(jnp.int32)
    own, xh, xl = factor_corner(place, corner)
    out = finish(place, xh, xl, row_raw, col_raw, own, assembled)
    return out.reshape(rows_local, 1, TILE, cols_local, 1, TILE)


def solution(mesh):
    in_specs = (
        P(None, "row", None, None, "col", None),
        P(("row", "col"), None, None),
        P(("row", "col"), None),
    )
    out_specs = P(None, "row", None, None, "col", None)
    return jax.shard_map(
        per_device, mesh=mesh, in_specs=in_specs, out_specs=out_specs, check_vma=False
    )
```

```python
import functools
import numpy as np
import jax
import jax.numpy as jnp
from jax import lax
from jax.experimental import pallas as pl
from jax.experimental.pallas import tpu as pltpu
from jax.sharding import PartitionSpec as P

CAP = 2
HEAD = 16
PANEL = 2048
TILE = 128
NT_DIMS = (((1,), (1,)), ((), ()))
SLOTS = 32


def split2(x):
    hi = x.astype(jnp.bfloat16)
    lo = (x - hi.astype(jnp.float32)).astype(jnp.bfloat16)
    return hi, lo


def nt(a, b):
    return lax.dot_general(a, b, NT_DIMS, preferred_element_type=jnp.float32)


def spread8(x):
    return jnp.broadcast_to(x, (8, TILE))


def total(terms):
    acc = terms[0]
    for term in terms[1:]:
        acc = acc + term
    return acc


def invert_tile(a_ref, i_ref, s_ref, out_ref, beside):
    row = lax.broadcasted_iota(jnp.int32, (TILE, TILE), 0)
    col = lax.broadcasted_iota(jnp.int32, (TILE, TILE), 1)
    i_ref[...] = (row == col).astype(jnp.float32)
    steps = TILE // 8
    for g in range(steps):
        base = 8 * g
        group = a_ref[base : base + 8, :]
        for k in range(8):
            s_ref[8 * k : 8 * k + 8, :] = spread8(group[:, base + k : base + k + 1])
        d = {}
        for k in range(8):
            for i in range(k, 8):
                d[i, k] = spread8(s_ref[8 * k + i : 8 * k + i + 1, :])
        ga = [spread8(a_ref[base + j : base + j + 1, :]) for j in range(8)]
        gi = [spread8(i_ref[base + j : base + j + 1, :]) for j in range(8)]
        rs = {}
        lo = {}
        for j in range(0, 8, 2):
            rs[j] = lax.rsqrt(d[j, j])
            det = lax.rsqrt(d[j, j] * d[j + 1, j + 1] - d[j + 1, j] * d[j + 1, j])
            rs[j + 1] = det * (d[j, j] * rs[j])
            lo[j + 1, j] = d[j + 1, j] * rs[j]
            for i in range(j + 2, 8):
                lo[i, j] = d[i, j] * rs[j]
                lo[i, j + 1] = (d[i, j + 1] - lo[i, j] * lo[j + 1, j]) * rs[j + 1]
            for k in range(j + 2, 8):
                for i in range(k, 8):
                    d[i, k] = d[i, k] - (lo[i, j] * lo[k, j] + lo[i, j + 1] * lo[k, j + 1])
        t = {}
        for j in range(8):
            t[j, j] = rs[j]
            for m in range(j):
                t[j, m] = -(total([lo[j, k] * t[k, m] for k in range(m, j)]) * rs[j])
        ui = [total([t[i, j] * gi[j] for j in range(i + 1)]) for i in range(8)]
        for i in range(8):
            out_ref[base + i : base + i + 1, :] = ui[i][0:1, :]
        if g < steps - 1:
            ua = [total([t[i, j] * ga[j] for j in range(i + 1)]) for i in range(8)]
            va = [total([t[i, j] * ua[i] for i in range(j, 8)]) for j in range(8)]
            vi = [total([t[i, j] * ui[i] for i in range(j, 8)]) for j in range(8)]
        for h in range(g + 1, steps):
            rows = slice(8 * h, 8 * h + 8)
            block = a_ref[rows, :]
            acc_a = block
            acc_i = i_ref[rows, :]
            for j in range(8):
                c = spread8(block[:, base + j : base + j + 1])
                acc_a = acc_a - c * va[j]
                acc_i = acc_i - c * vi[j]
            a_ref[rows, :] = acc_a
            i_ref[rows, :] = acc_i
        beside(g)


def unit_table(first, last):
    pairs = PANEL // 256
    table = np.full((pairs, SLOTS), (pairs - first) * 8, np.int32)
    for p in range(max(first, 1), last):
        units = [(q - first) * 8 + b for q in range(p + 1, pairs) for b in range(pairs) if b <= p - 1 or b >= q]
        table[p, : len(units)] = units
    return table.reshape(-1)


def factor_kernel(first, last, place_ref, unit_ref, *rest):
    tiles = PANEL // TILE
    pairs = tiles // 2
    source_ref, own_ref, xh_ref, xl_ref, *rest = rest
    m_ref, eh_ref, el_ref, a_ref, o_ref, i_ref, s_ref, t_ref, sem = rest
    for j in range(tiles):
        for i in range(tiles):
            spot = (j // 2, slice(i * TILE, (i + 1) * TILE), slice(j % 2 * TILE, (j % 2 + 1) * TILE))
            if i >= j:
                m_ref[spot] = source_ref[i % 8 * 16 + j, i // 8].astype(jnp.float32)
            else:
                m_ref[spot] = jnp.zeros((TILE, TILE), jnp.float32)
    own_ref[...] = jnp.zeros_like(own_ref)
    r = place_ref[0]
    c = place_ref[1]
    row = lax.broadcasted_iota(jnp.int32, (TILE, TILE), 0)
    col = lax.broadcasted_iota(jnp.int32, (TILE, TILE), 1)
    identity = (row == col).astype(jnp.float32)
    zero = jnp.zeros((TILE, TILE), jnp.bfloat16)

    def product(rows, cols, buf):
        lh, ll = eh_ref[buf, rows, :], el_ref[buf, rows, :]
        rh, rl = eh_ref[buf, cols, :], el_ref[buf, cols, :]
        return nt(lh, rh) + nt(lh, rl) + nt(ll, rh)

    def block_rows(b):
        return pl.ds(pl.multiple_of(b * 256, 256), 256)

    def tile_rows(i):
        return pl.ds(pl.multiple_of(i * TILE, TILE), TILE)

    def apply(code, buf):
        q = code // 8
        rows = block_rows(code % 8)
        cols = block_rows(jnp.minimum(q + first, pairs - 1))
        m_ref[q, rows, :] = m_ref[q, rows, :] - product(rows, cols, buf)

    def times(x, y):
        xh, xl = x
        yh, yl = y
        parts = nt(
            jnp.concatenate([xh, xl], 1),
            jnp.concatenate([jnp.concatenate([yh, yh], 1), jnp.concatenate([yl, yl], 1)], 0),
        )
        return parts[:, :TILE] + parts[:, TILE:]

    def keep_own(k, buf, half):
        @pl.when(k == c)
        def _():
            diag = times(split2(o_ref[...]), split2(t_ref[...]))
            diag = jnp.where(row >= col, diag, 0.0).astype(jnp.bfloat16)
            for a in range(2):
                i = r + a * 8
                src = eh_ref[buf, tile_rows(i), half * TILE : (half + 1) * TILE]
                own_ref[a] = jnp.where(i == k, diag, jnp.where(i > k, src, zero))

    def column(p, buf, half):
        inverse = split2(t_ref[...])
        lanes = slice(half * TILE, (half + 1) * TILE)
        for b in range(pairs):
            rows = slice(b * 256, (b + 1) * 256)
            eh, el = split2(times(split2(m_ref[p - first, rows, lanes]), inverse))
            eh_ref[buf, rows, lanes] = eh
            el_ref[buf, rows, lanes] = el

    def keep_inverse(p, buf):
        wide = pl.ds(pl.multiple_of(p * 256, 256), 256)
        return (
            pltpu.make_async_copy(eh_ref.at[buf], xh_ref.at[:, wide], sem.at[0, buf]),
            pltpu.make_async_copy(el_ref.at[buf], xl_ref.at[:, wide], sem.at[1, buf]),
        )

    def step(p, carry):
        local = p - first
        buf = p % 2
        old = 1 - buf
        k = 2 * p
        m_ref[local, tile_rows(k), TILE:] = jnp.zeros((TILE, TILE), jnp.float32)

        diag = m_ref[local, tile_rows(k), 0:TILE]
        diag = jnp.where(p > 0, diag - product(tile_rows(k), tile_rows(k), old), diag)
        a_ref[...] = diag
        o_ref[...] = diag

        def first_beside(g):
            if g < 8:
                rows = slice(g * 256, (g + 1) * 256)
                old_block = m_ref[local, rows, :]
                new_block = old_block - product(rows, block_rows(p), old)
                m_ref[local, rows, :] = jnp.where(p > 0, new_block, old_block)
            else:
                apply(unit_ref[p * SLOTS + g - 8], old)

        invert_tile(a_ref, i_ref, s_ref, t_ref, first_beside)
        m_ref[local, tile_rows(k), 0:TILE] = identity
        m_ref[local, tile_rows(k), TILE:] = jnp.zeros((TILE, TILE), jnp.float32)
        @pl.when(p >= 2)
        def _():
            for copy in keep_inverse(p - 2, buf):
                copy.wait()

        column(p, buf, 0)
        keep_own(k, buf, 0)

        def pair_product(rows):
            lanes = slice(0, TILE)
            return times(
                (eh_ref[buf, rows, lanes], el_ref[buf, rows, lanes]),
                (eh_ref[buf, tile_rows(k + 1), lanes], el_ref[buf, tile_rows(k + 1), lanes]),
            )

        diag = m_ref[local, tile_rows(k + 1), TILE:] - pair_product(tile_rows(k + 1))
        a_ref[...] = diag
        o_ref[...] = diag

        def second_beside(g):
            if g < 8:
                rows = slice(g * 256, (g + 1) * 256)
                m_ref[local, rows, TILE:] = m_ref[local, rows, TILE:] - pair_product(rows)
            apply(unit_ref[p * SLOTS + 8 + g], old)
            if g >= 12:
                apply(unit_ref[p * SLOTS + 12 + g], old)

        invert_tile(a_ref, i_ref, s_ref, t_ref, second_beside)
        m_ref[local, tile_rows(k + 1), TILE:] = identity
        column(p, buf, 1)
        keep_own(k + 1, buf, 1)
        eh_ref[buf, tile_rows(k + 1), 0:TILE] = zero
        el_ref[buf, tile_rows(k + 1), 0:TILE] = zero
        for copy in keep_inverse(p, buf):
            copy.start()
        return carry

    lax.fori_loop(first, last, step, 0)
    for p in (pairs - 2, pairs - 1):
        for copy in keep_inverse(p, p % 2):
            copy.wait()


def factor_corner(place, corner):
    pairs = PANEL // 256
    vm = pl.BlockSpec(memory_space=pltpu.VMEM)
    hbm = pl.BlockSpec(memory_space=pl.ANY)
    smem = pl.BlockSpec(memory_space=pltpu.SMEM)
    tile = pltpu.VMEM((TILE, TILE), jnp.float32)
    return pl.pallas_call(
        functools.partial(factor_kernel, 0, pairs),
        out_shape=(
            jax.ShapeDtypeStruct((2, TILE, TILE), jnp.bfloat16),
            jax.ShapeDtypeStruct((PANEL, PANEL), jnp.bfloat16),
            jax.ShapeDtypeStruct((PANEL, PANEL), jnp.bfloat16),
        ),
        in_specs=[smem, smem, vm],
        out_specs=(vm, hbm, hbm),
        scratch_shapes=[
            pltpu.VMEM((pairs + 1, PANEL, 256), jnp.float32),
            pltpu.VMEM((2, PANEL, 256), jnp.bfloat16),
            pltpu.VMEM((2, PANEL, 256), jnp.bfloat16),
            tile,
            tile,
            tile,
            tile,
            tile,
            pltpu.SemaphoreType.DMA((2, 2)),
        ],
        compiler_params=pltpu.CompilerParams(vmem_limit_bytes=56 * 1024 * 1024),
        cost_estimate=pl.CostEstimate(flops=90_000_000_000, bytes_accessed=24_000_000, transcendentals=0),
        name="factor_corner",
    )(place, jnp.asarray(unit_table(0, pairs)), corner)


def pack_kernel(slot_ref, child_ref, head_ref, packed_ref):
    packed_ref[:, CAP * TILE :, :] = head_ref[...]

    def move(t, carry):
        slot = slot_ref[t]
        rows = pl.ds(pl.multiple_of(slot % CAP * TILE, TILE), TILE)
        packed_ref[slot // CAP, rows, :] = child_ref[t]
        return carry

    lax.fori_loop(0, child_ref.shape[0], move, 0)


def pack(slots, child_tiles, head):
    vm = pl.BlockSpec(memory_space=pltpu.VMEM)
    return pl.pallas_call(
        pack_kernel,
        out_shape=jax.ShapeDtypeStruct((head.shape[0], CAP * TILE + HEAD, TILE), jnp.bfloat16),
        in_specs=[pl.BlockSpec(memory_space=pltpu.SMEM), vm, vm],
        out_specs=vm,
        compiler_params=pltpu.CompilerParams(vmem_limit_bytes=32 * 1024 * 1024),
        cost_estimate=pl.CostEstimate(flops=0, bytes_accessed=16_000_000, transcendentals=0),
        name="pack_tiles",
    )(slots, child_tiles, head)


def extend_kernel(id_ref, front_ref, arrived_ref, out_ref, panel_ref, acc_ref):
    cols_local = front_ref.shape[1] // TILE
    rows_local = front_ref.shape[0]
    acc_ref[0:rows_local, :] = front_ref[...].astype(jnp.float32)

    def add(s, carry):
        local = id_ref[s]
        used = local >= 0
        top = jnp.where(used, local // cols_local * TILE, rows_local)
        left = jnp.where(used, local % cols_local * TILE, 0)
        spot = (pl.ds(pl.multiple_of(top, TILE), TILE), pl.ds(pl.multiple_of(left, TILE), TILE))
        rows = pl.ds(pl.multiple_of(s % CAP * TILE, TILE), TILE)
        acc_ref[spot] = acc_ref[spot] + arrived_ref[s // CAP, rows, :].astype(jnp.float32)
        return carry

    lax.fori_loop(0, CAP * arrived_ref.shape[0], add, 0, unroll=4)
    summed = acc_ref[0:rows_local, :].astype(jnp.bfloat16)
    out_ref[...] = summed
    panel_ref[...] = summed[2 * TILE :, 0:TILE]


def extend(ids, front, arrived):
    vm = pl.BlockSpec(memory_space=pltpu.VMEM)
    return pl.pallas_call(
        extend_kernel,
        out_shape=(
            jax.ShapeDtypeStruct(front.shape, jnp.bfloat16),
            jax.ShapeDtypeStruct((front.shape[0] - 2 * TILE, TILE), jnp.bfloat16),
        ),
        in_specs=[pl.BlockSpec(memory_space=pltpu.SMEM), vm, vm],
        out_specs=(vm, vm),
        scratch_shapes=[pltpu.VMEM((front.shape[0] + TILE, front.shape[1]), jnp.float32)],
        compiler_params=pltpu.CompilerParams(vmem_limit_bytes=48 * 1024 * 1024),
        cost_estimate=pl.CostEstimate(flops=10_000_000, bytes_accessed=30_000_000, transcendentals=0),
        name="extend_add",
    )(ids, front, arrived)


def finish_kernel(
    place_ref, xh_ref, xl_ref, row_ref, col_ref, own_ref, assembled_ref, out_ref, a_ref, p_ref, sum_ref, acc_ref
):
    step = pl.program_id(0)
    steps = PANEL // (2 * TILE)
    rows_low = row_ref.shape[1] * TILE
    cols_low = col_ref.shape[1] * TILE
    total = rows_low + cols_low
    cols_local = assembled_ref.shape[1] // TILE
    c = place_ref[1]
    width = 2 * TILE

    @pl.when(step == 0)
    def _():
        top = 2 * TILE * cols_local
        out_ref[0:top, :] = jnp.zeros((top, TILE), jnp.float32)
        for a in range(2):
            rows = pl.ds(a * TILE * cols_local, TILE, stride=cols_local)
            out_ref[rows, :] = own_ref[a].astype(jnp.float32)
        acc_ref[...] = assembled_ref[2 * TILE :, TILE:].astype(jnp.float32)

    for piece in range(2):
        lanes = slice(piece * TILE, (piece + 1) * TILE)
        a_ref[step, 0:rows_low, lanes] = row_ref[piece].reshape(rows_low, TILE)
        a_ref[step, rows_low:total, lanes] = col_ref[piece].reshape(cols_low, TILE)

    def part(first, count):
        rows = pl.ds(pl.multiple_of(first * width, width), count * width)
        a = jnp.concatenate([a_ref[first + n] for n in range(count)], 1)
        return jnp.dot(a, xh_ref[rows, :], preferred_element_type=jnp.float32) + jnp.dot(
            a, xl_ref[rows, :], preferred_element_type=jnp.float32
        )

    odd = (step + 1) % 2

    @pl.when(odd == 1)
    def _():
        sum_ref[...] = part(0, 1)

    @pl.when(odd == 0)
    def _():
        sum_ref[...] = jnp.zeros_like(sum_ref)

    def solve(n, carry):
        sum_ref[...] = sum_ref[...] + part(odd + 2 * n, 2)
        return carry

    lax.fori_loop(0, (step + 1) // 2, solve, 0)
    p_ref[:, pl.ds(pl.multiple_of(step % 2 * width, width), width)] = sum_ref[...].astype(jnp.bfloat16)

    @pl.when(step == c // 2)
    def _():
        lane = pl.multiple_of(c % 4 * TILE, TILE)
        rows = pl.ds(2 * TILE * cols_local, rows_low, stride=cols_local)
        out_ref[rows, :] = p_ref[0:rows_low, pl.ds(lane, TILE)].astype(jnp.float32)

    def update(b, carry):
        rows = pl.ds(pl.multiple_of(b * chunk, chunk), chunk)
        acc_ref[rows, :] = acc_ref[rows, :] - nt(p_ref[rows, :], p_ref[rows_low:total, :])
        return carry

    chunk = rows_low

    @pl.when(step % 2 == 1)
    def _():
        lax.fori_loop(0, 1, update, 0)

    @pl.when(step == steps - 1)
    def _():
        def write(t, carry):
            lanes = pl.ds(pl.multiple_of((t - 1) * TILE, TILE), TILE)
            out_ref[pl.ds(2 * TILE * cols_local + t, rows_low, stride=cols_local), :] = acc_ref[:, lanes]
            return carry

        lax.fori_loop(1, cols_local, write, 0)


def finish(place, xh, xl, row_raw, col_raw, own, assembled):
    width = 2 * TILE
    steps = PANEL // width
    tiles_row = row_raw.shape[1]
    tiles_col = col_raw.shape[1]
    total = (tiles_row + tiles_col) * TILE
    vm = pl.BlockSpec(memory_space=pltpu.VMEM)
    inverse = pl.BlockSpec((PANEL, width), lambda s: (0, s))
    return pl.pallas_call(
        finish_kernel,
        grid=(steps,),
        out_shape=jax.ShapeDtypeStruct((assembled.shape[0] * assembled.shape[1] // TILE, TILE), jnp.float32),
        in_specs=[
            pl.BlockSpec(memory_space=pltpu.SMEM),
            inverse,
            inverse,
            pl.BlockSpec((2, tiles_row, TILE, TILE), lambda s: (s, 0, 0, 0)),
            pl.BlockSpec((2, tiles_col, TILE, TILE), lambda s: (s, 0, 0, 0)),
            vm,
            vm,
        ],
        out_specs=vm,
        scratch_shapes=[
            pltpu.VMEM((steps, total, width), jnp.bfloat16),
            pltpu.VMEM((total, 2 * width), jnp.bfloat16),
            pltpu.VMEM((total, width), jnp.float32),
            pltpu.VMEM((tiles_row * TILE, tiles_col * TILE), jnp.float32),
        ],
        compiler_params=pltpu.CompilerParams(
            vmem_limit_bytes=56 * 1024 * 1024, dimension_semantics=("arbitrary",)
        ),
        cost_estimate=pl.CostEstimate(flops=40_000_000_000, bytes_accessed=50_000_000, transcendentals=0),
        name="solve_update",
    )(place, xh, xl, row_raw, col_raw, own, assembled)


def per_device(front, child_tiles, tile_map):
    rows_local = front.shape[0]
    cols_local = front.shape[3]
    row_count = lax.axis_size("row")
    col_count = lax.axis_size("col")
    device_count = row_count * col_count
    row_index = lax.axis_index("row")
    col_index = lax.axis_index("col")
    both = ("row", "col")
    corner = front[0:2, 0, :, 0, 0, :]
    corner = lax.all_gather(corner, both, axis=0, tiled=False)

    owners = tile_map[:, 0] % row_count * col_count + tile_map[:, 1] % col_count
    local_ids = tile_map[:, 0] // row_count * cols_local + tile_map[:, 1] // col_count
    owner_hits = (owners[:, None] == jnp.arange(device_count)[None, :]).astype(jnp.int32)
    slot_rank = jnp.sum(jnp.cumsum(owner_hits, 0) * owner_hits, 1) - 1
    slot_index = owners * CAP + slot_rank
    targets = jnp.full((device_count * CAP,), -1, jnp.int32).at[slot_index].set(local_ids)
    head = jnp.pad(
        targets.astype(jnp.bfloat16).reshape(device_count, 1, CAP), ((0, 0), (0, HEAD - 1), (0, TILE - CAP))
    )
    flat_front = front.reshape(rows_local * TILE, cols_local * TILE)
    packed, flat_front = lax.optimization_barrier((pack(slot_index, child_tiles, head), flat_front))
    arrived = lax.all_to_all(packed, both, split_axis=0, concat_axis=0, tiled=True)
    arrived_ids = arrived[:, CAP * TILE, 0:CAP].astype(jnp.int32).reshape(device_count * CAP)
    assembled, panel = extend(arrived_ids, flat_front, arrived)
    low_tiles = rows_local - 2
    panel = panel.reshape(low_tiles, TILE, TILE)
    row_raw = lax.all_gather(panel, "col", axis=0, tiled=False)
    split_panel = panel.reshape(low_tiles // 2, 2, TILE, TILE)
    halves = (split_panel[:, 0], split_panel[:, 1])
    parity = col_index % 2
    received = []
    for k in range(2):
        pairs = []
        for r in range(row_count):
            for c in range(col_count):
                h = (c % 2) ^ k
                pairs.append((r * col_count + c, (c // 2) * col_count + row_count * h + r))
        outgoing = jnp.where(parity == k, halves[0], halves[1])
        received.append(lax.ppermute(outgoing, both, pairs))
    high = col_index // row_count
    first = jnp.where(high == 0, received[0], received[1])
    second = jnp.where(high == 0, received[1], received[0])
    pieces = jnp.broadcast_to(jnp.stack([first, second]), (row_count, 2) + first.shape)
    corner, pieces = lax.optimization_barrier((corner, pieces))
    col_raw = lax.all_to_all(
        pieces, "row", split_axis=0, concat_axis=0, tiled=True
    ).reshape(col_count, low_tiles // 2, TILE, TILE)
    place = jnp.stack([row_index, col_index]).astype(jnp.int32)
    own, xh, xl = factor_corner(place, corner)
    out = finish(place, xh, xl, row_raw, col_raw, own, assembled)
    return out.reshape(rows_local, 1, TILE, cols_local, 1, TILE)


def solution(mesh):
    in_specs = (
        P(None, "row", None, None, "col", None),
        P(("row", "col"), None, None),
        P(("row", "col"), None),
    )
    out_specs = P(None, "row", None, None, "col", None)
    return jax.shard_map(
        per_device, mesh=mesh, in_specs=in_specs, out_specs=out_specs, check_vma=False
    )
```
